256 devices in a mesh: seq: 64 (over x, y_lo, z), chan: 4 (over y_hi, core).
Axes of the slice: x: 4, y: 4 (y_hi: 2, y_lo: 2; y = y_hi * 2 + y_lo), z: 8, core: 2. Of those that a mesh axis runs over, the one named last changes fastest.
Arguments:
- q_stream: bfloat16 [8192, 2048], P('seq', 'chan'), may hold values from -6 to 6
- k_stream: bfloat16 [8192, 2048], P('seq', 'chan'), may hold values from -6 to 6
- v_stream: bfloat16 [8192, 2048], P('seq', 'chan'), may hold values from -6 to 6
- short_taps: float32 [3, 3, 2048], P(None, None, 'chan'), may hold values from -3.5 to 3.5
- long_filter: float32 [8192, 2048], P('seq', 'chan'), may hold values from -2 to 2
- skip_gain: float32 [2048], P('chan'), may hold values from -6 to 6
- out_weight: bfloat16 [2048, 4096], P('chan'), may hold values from -0.1875 to 0.1875
Outputs:
- mixed_out: bfloat16 [8192, 4096], P('seq', 'chan')
The draws below stay inside these ranges and needn't reach their ends.
All inputs are finite; a program needn't handle non-finite values.
Results may differ from the reference program's by a relative error of at most 0.0095.
Values may be sent and summed in bfloat16 or wider, within the bound.
A program may use at most 64 MiB of HBM per device.

```python
import math
import jax
import jax.numpy as jnp

D = 4096
TAPS = 3
SEQUENCE_LENGTH = 8192
OPERATOR_WIDTH = 2048


def draw_long_filter(key, part):
    key = jax.random.fold_in(key, 7)
    decay_scale_key, picker_random_key, spike_random_key, retain_random_key, noise_random_key = jax.random.split(key, 5)
    delay_values = jnp.arange(SEQUENCE_LENGTH, dtype=jnp.float32)[:, None]
    selector = jax.random.randint(picker_random_key, (OPERATOR_WIDTH,), 0, 20)
    uniform_draw = jax.random.uniform(decay_scale_key, (OPERATOR_WIDTH,), dtype=jnp.float32)
    fast_scale = 8.0 * jnp.exp(uniform_draw * math.log(5.0))
    slow_scale = 2.0 * SEQUENCE_LENGTH * jnp.exp(uniform_draw * math.log(3.0))
    slow_channel = selector < 10
    slow_envelope = jnp.exp(-delay_values / slow_scale) * jnp.sqrt(2.0 / slow_scale)
    fast_envelope = jnp.exp(-delay_values / fast_scale) * jnp.sqrt(2.0 / fast_scale)
    base_envelope = jnp.where(slow_channel[None, :], slow_envelope, fast_envelope + 0.6 * slow_envelope)
    spike_rows = jax.random.randint(spike_random_key, (3,), 0, SEQUENCE_LENGTH)
    filter_row_index = jnp.arange(SEQUENCE_LENGTH, dtype=jnp.int32)[:, None]
    spike_count = jnp.sum((filter_row_index >= spike_rows[None, :]).astype(jnp.float32), axis=1)[:, None]
    spike_keep_mask = jax.random.uniform(retain_random_key, (OPERATOR_WIDTH,), minval=0.6, maxval=0.8)
    decay_envelope = base_envelope * spike_keep_mask ** spike_count
    rough_part = jnp.clip(jax.random.normal(noise_random_key, (SEQUENCE_LENGTH, OPERATOR_WIDTH), dtype=jnp.float32), -3.8, 3.8)
    return jnp.clip(rough_part * decay_envelope, -2.0, 2.0).astype(jnp.float32)


def raised(array, own_key, source, target, blocks, factor):
    owner, partner = [(jnp.arange(array.shape[dim]) // (array.shape[dim] // blocks)).reshape([-1 if axis == dim else 1 for axis in range(array.ndim)]) for dim in (source, target)]
    chosen = jax.random.permutation(own_key, blocks)[partner]
    strong = (owner == chosen) | (owner == (partner + blocks // 2) % blocks)
    return jnp.where(strong, factor * array, array)


def steps_of(rng, shape, cuts, least, high):
    loudness = 1.0
    for position, parts in cuts:
        heights = jax.random.uniform(jax.random.fold_in(jax.random.fold_in(rng, 6), position), (parts,), jnp.float32, least / len(cuts), high / len(cuts))
        loudness = loudness * jnp.repeat(jnp.exp(heights), shape[position] // parts).reshape((-1,) + (1,) * (len(shape) - 1 - position))
    return loudness


def scatter_about(stream_key, extent, scale, most, cuts=(), kind=jnp.bfloat16):
    factor_of = steps_of(stream_key, extent, cuts, -0.22, 0.18) if cuts else 1.0
    entries = jax.random.normal(stream_key, extent, jnp.float32) * scale * factor_of
    return jnp.minimum(jnp.maximum(entries, -most), most).astype(kind)


def bell_draw_with(own_key, shape, spread, limit, cuts, heavy, kind=jnp.bfloat16):
    values = spread * jax.random.normal(own_key, shape, jnp.float32)
    if cuts:
        values = values * steps_of(own_key, shape, cuts, -0.22, 0.18)
    return jnp.clip(raised(values, jax.random.fold_in(own_key, 3), *heavy), -limit, limit).astype(kind)


def setup_inputs(seed: int = 0) -> dict:
    key_of = jax.random.split(jax.random.key(seed), 8)
    return {
        "q_stream": scatter_about(key_of[0], (SEQUENCE_LENGTH, OPERATOR_WIDTH), 1.0, 6.0, ((0, 64), (1, 4))),
        "k_stream": scatter_about(key_of[1], (SEQUENCE_LENGTH, OPERATOR_WIDTH), 1.0, 6.0, ((0, 64), (1, 4))),
        "v_stream": scatter_about(key_of[2], (SEQUENCE_LENGTH, OPERATOR_WIDTH), 1.0, 6.0, ((0, 64), (1, 4))),
        "short_taps": scatter_about(key_of[3], (3, TAPS, OPERATOR_WIDTH), 0.6, 3.5, ((2, 4),), jnp.float32),
        "long_filter": draw_long_filter(jax.random.fold_in(key_of[7], 71), 0),
        "skip_gain": scatter_about(key_of[5], (OPERATOR_WIDTH,), 1.0, 6.0, ((0, 4),), jnp.float32),
        "out_weight": bell_draw_with(key_of[6], (OPERATOR_WIDTH, D), OPERATOR_WIDTH ** -0.5, 0.1875, ((0, 4),), (0, 1, 4, 2.0)),
    }


def short_filter(stream, tap_weights):
    values = stream.astype(jnp.float32)
    rim_rows = tap_weights.shape[0] - 1
    length = values.shape[0]
    padded = jnp.pad(values, ((rim_rows, 0), (0, 0)))
    result = jnp.zeros_like(values)
    for lag_index in range(tap_weights.shape[0]):
        result = result + tap_weights[lag_index] * padded[rim_rows - lag_index: rim_rows - lag_index + length]
    return result


def reference(q_stream, k_stream, v_stream, short_taps, long_filter, skip_gain, out_weight):
    q_short = short_filter(q_stream, short_taps[0])
    k_short = short_filter(k_stream, short_taps[1])
    v_short = short_filter(v_stream, short_taps[2])
    product = k_short * v_short
    length = product.shape[0]
    spectrum = jnp.fft.rfft(product, n=2 * length, axis=0) * jnp.fft.rfft(long_filter, n=2 * length, axis=0)
    convolved = jnp.fft.irfft(spectrum, n=2 * length, axis=0)[:length].astype(jnp.float32)
    gated_values = (q_short * (convolved + skip_gain * product)).astype(jnp.bfloat16)
    return jnp.dot(gated_values, out_weight, preferred_element_type=jnp.float32).astype(jnp.bfloat16)
```

```python
import functools
import math

import jax
import jax.numpy as jnp
import ml_dtypes
import numpy as np
from jax import lax
from jax.experimental import pallas as pl
from jax.experimental.pallas import tpu as pltpu
from jax.sharding import PartitionSpec as P

MESH = pl.DeviceIdType.MESH
F32 = jnp.float32
BF16 = jnp.bfloat16
HALO = 16
PARTS = 4


def transform_tables(blocks, tokens, group):
    length = blocks * tokens
    frequency = np.arange(blocks) + 0.25
    outer_angle = 2 * math.pi * np.outer(frequency, np.arange(blocks)) / blocks
    outer = np.stack([np.cos(outer_angle), np.sin(outer_angle)], axis=1).reshape(2 * blocks, blocks)
    first = np.kron(outer, np.eye(group))
    turn = 2 * math.pi * np.outer(frequency, np.arange(tokens)) / length
    turn = np.repeat(turn, group, axis=0)
    inner_angle = 2 * math.pi * np.outer(np.arange(tokens), np.arange(tokens)) / tokens
    cosine, sine = np.cos(inner_angle), np.sin(inner_angle)
    inner = np.block([[cosine, sine], [-sine, cosine]])
    back = np.block([[cosine, -sine], [sine, cosine]]) / length
    narrow = lambda table: table.astype(ml_dtypes.bfloat16)
    return (
        narrow(first),
        narrow(first.T.copy()),
        narrow(inner),
        narrow(back),
        np.cos(turn).astype(np.float32),
        np.sin(turn).astype(np.float32),
    )


def dot(a, b):
    return jnp.dot(a, b, preferred_element_type=F32)


def kernel(
    n,
    q_hbm,
    k_hbm,
    v_hbm,
    taps_hbm,
    filter_hbm,
    skip_hbm,
    weight_hbm,
    first_hbm,
    last_hbm,
    inner_hbm,
    back_hbm,
    cos_hbm,
    sin_hbm,
    out_ref,
    streams,
    taps,
    filt,
    skip,
    weight,
    first,
    last,
    inner,
    back,
    cosine,
    sine,
    halo,
    padded,
    q_short,
    skipped,
    send_h,
    send_p,
    send_y,
    recv_h,
    recv_p,
    recv_y,
    response,
    send_core,
    recv_core,
    send_cross,
    recv_cross,
    load_sem,
    halo_send,
    halo_recv,
    all_send,
    all_recv,
    core_send,
    core_recv,
    cross_send,
    cross_recv,
):
    me, chan = lax.axis_index("seq"), lax.axis_index("chan")
    core, high = lax.rem(chan, 2), lax.div(chan, 2)
    other_core = high * 2 + 1 - core
    other_high = (1 - high) * 2 + core
    tokens, channels = filt.shape
    group = channels // n
    columns = weight.shape[2]

    def block_of(y_high, y_core):
        return weight_hbm.at[:, pl.ds(pl.multiple_of((y_high * 2 + y_core) * columns, columns), columns)]

    pairs = [
        (filter_hbm, filt),
        (k_hbm, streams.at[1]),
        (v_hbm, streams.at[2]),
        (q_hbm, streams.at[0]),
        (taps_hbm, taps),
        (skip_hbm, skip),
        (first_hbm, first),
        (cos_hbm, cosine),
        (sin_hbm, sine),
        (inner_hbm, inner),
        (back_hbm, back),
        (last_hbm, last),
        (block_of(1 - high, 1 - core), weight.at[0]),
        (block_of(1 - high, core), weight.at[1]),
        (block_of(high, 1 - core), weight.at[2]),
        (block_of(high, core), weight.at[3]),
    ]
    loads = [pltpu.make_async_copy(src, dst, load_sem.at[i]) for i, (src, dst) in enumerate(pairs)]
    for load in loads[:4]:
        load.start()

    barrier = pltpu.get_barrier_semaphore()

    @pl.loop(1, n)
    def _(d):
        pl.semaphore_signal(barrier, inc=1, device_id=(lax.rem(me + d, n), chan), device_id_type=MESH)

    pl.semaphore_signal(barrier, inc=1, device_id=(me, other_core), device_id_type=MESH)
    pl.semaphore_signal(barrier, inc=1, device_id=(me, other_high), device_id_type=MESH)
    for load in loads[4:]:
        load.start()

    def exchange(source, target, index):
        @pl.loop(1, n)
        def _(d):
            peer = lax.rem(me + d, n)
            pltpu.make_async_remote_copy(
                src_ref=source.at[peer],
                dst_ref=target.at[me],
                send_sem=all_send.at[index],
                recv_sem=all_recv.at[index],
                device_id=(peer, chan),
                device_id_type=MESH,
            ).start()

        target[me] = source[me]

    def arrived(buffer, index):
        part = buffer.at[pl.ds(0, n - 1)]
        pltpu.make_async_copy(part, part, all_recv.at[index]).wait()

    def left(buffer, index):
        part = buffer.at[pl.ds(0, n - 1)]
        pltpu.make_async_copy(part, part, all_send.at[index]).wait()

    def to_channels(value, buffer):
        per = tokens // group
        for i in range(channels // tokens):
            turned = value[:, i * tokens : (i + 1) * tokens].T
            buffer[i * per : (i + 1) * per] = turned.reshape(per, group, tokens).astype(BF16)

    loads[0].wait()
    to_channels(filt[...], send_h)
    for load in loads[1:4]:
        load.wait()

    pl.semaphore_wait(barrier, n + 1)
    after = lax.rem(me + 1, n)
    rims = []
    for i in (1, 2, 0):
        rims.append(
            pltpu.make_async_remote_copy(
                src_ref=streams.at[i, pl.ds(tokens - HALO, HALO)],
                dst_ref=halo.at[i],
                send_sem=halo_send.at[i],
                recv_sem=halo_recv.at[i],
                device_id=(after, chan),
                device_id_type=MESH,
            )
        )
        rims[-1].start()
    exchange(send_h, recv_h, 0)

    for load in loads[4:6]:
        load.wait()
    inside = jnp.where(me > 0, 1.0, 0.0).astype(F32)

    def short(i):
        padded[0:HALO] = halo[i].astype(F32) * inside
        padded[HALO : HALO + tokens] = streams[i].astype(F32)
        total = taps[i, 0:1] * padded[HALO : HALO + tokens]
        for lag in range(1, taps.shape[1]):
            total += taps[i, lag : lag + 1] * padded[HALO - lag : HALO - lag + tokens]
        return total

    rims[0].wait_recv()
    rims[1].wait_recv()
    k_short = short(1)
    product = k_short * short(2)
    to_channels(product, send_p)
    exchange(send_p, recv_p, 1)
    skipped[...] = skip[...] * product
    rims[2].wait_recv()
    q_short[...] = short(0)

    for load in loads[6:]:
        load.wait()

    def split(value):
        value = value.reshape(n, 2, group, tokens)
        return value[:, 0].reshape(channels, tokens), value[:, 1].reshape(channels, tokens)

    def forward(buffer):
        signal = buffer[...].astype(F32).reshape(channels, tokens).astype(BF16)
        real, imag = split(dot(first[...], signal))
        turned = [real * cosine[...] - imag * sine[...], real * sine[...] + imag * cosine[...]]
        return dot(jnp.concatenate(turned, axis=1).astype(BF16), inner[...])

    arrived(recv_h, 0)
    response[...] = forward(recv_h)
    arrived(recv_p, 1)
    spectrum = forward(recv_p)
    p_real, p_imag = spectrum[:, :tokens], spectrum[:, tokens:]
    h_real, h_imag = response[:, :tokens], response[:, tokens:]
    filtered = [p_real * h_real - p_imag * h_imag, p_real * h_imag + p_imag * h_real]
    mixed = dot(jnp.concatenate(filtered, axis=1).astype(BF16), back[...])
    real, imag = mixed[:, :tokens], mixed[:, tokens:]
    turned = [real * cosine[...] + imag * sine[...], imag * cosine[...] - real * sine[...]]
    turned = [part.reshape(n, 1, group, tokens) for part in turned]
    turned = jnp.concatenate(turned, axis=1).reshape(2 * channels, tokens).astype(BF16)
    convolved = dot(last[...], turned)
    send_y[...] = convolved.reshape(n, group, tokens).astype(BF16)
    exchange(send_y, recv_y, 2)
    arrived(recv_y, 2)

    long_part = recv_y[...].astype(F32).reshape(channels, tokens)
    long_part = jnp.concatenate([long_part[i * tokens : (i + 1) * tokens].T for i in range(channels // tokens)], axis=1)
    gated = (q_short[...] * (long_part + skipped[...])).astype(BF16)

    width = columns // PARTS

    def project(i, part):
        return dot(gated, weight[i, :, part * width : (part + 1) * width])

    def core_copy(half, part):
        return pltpu.make_async_remote_copy(
            src_ref=send_core.at[half, part],
            dst_ref=recv_core.at[half, part],
            send_sem=core_send.at[half, part],
            recv_sem=core_recv.at[half, part],
            device_id=(me, other_core),
            device_id_type=MESH,
        )

    def cross_copy(part):
        return pltpu.make_async_remote_copy(
            src_ref=send_cross.at[part],
            dst_ref=recv_cross.at[part],
            send_sem=cross_send.at[part],
            recv_sem=cross_recv.at[part],
            device_id=(me, other_high),
            device_id_type=MESH,
        )

    for part in range(PARTS):
        send_core[0, part] = project(0, part).astype(BF16)
        core_copy(0, part).start()
    for part in range(PARTS):
        mine = project(1, part)
        core_copy(0, part).wait_recv()
        send_cross[part] = (mine + recv_core[0, part].astype(F32)).astype(BF16)
        cross_copy(part).start()
    for part in range(PARTS):
        send_core[1, part] = project(2, part).astype(BF16)
        core_copy(1, part).start()
    for part in range(PARTS):
        mine = project(3, part)
        core_copy(1, part).wait_recv()
        mine = mine + recv_core[1, part].astype(F32)
        cross_copy(part).wait_recv()
        out_ref[:, part * width : (part + 1) * width] = (mine + recv_cross[part].astype(F32)).astype(BF16)

    for rim in rims:
        rim.wait_send()
    left(send_h, 0)
    left(send_p, 1)
    left(send_y, 2)
    for part in range(PARTS):
        core_copy(0, part).wait_send()
        core_copy(1, part).wait_send()
        cross_copy(part).wait_send()


def body(n, q_stream, k_stream, v_stream, short_taps, long_filter, skip_gain, out_weight):
    tokens, channels = long_filter.shape
    rows, features = out_weight.shape
    columns = features // lax.axis_size("chan")
    group = channels // n
    tables = transform_tables(n, tokens, group)
    hbm = pl.BlockSpec(memory_space=pl.ANY)
    width = columns // PARTS
    slabs = pltpu.VMEM((n, group, tokens), BF16)
    scratch = [
        pltpu.VMEM((3, tokens, channels), BF16),
        pltpu.VMEM(short_taps.shape, F32),
        pltpu.VMEM((tokens, channels), F32),
        pltpu.VMEM((1, channels), F32),
        pltpu.VMEM((4, rows, columns), BF16),
        *[pltpu.VMEM(table.shape, table.dtype) for table in tables],
        pltpu.VMEM((3, HALO, channels), BF16),
        pltpu.VMEM((HALO + tokens, channels), F32),
        pltpu.VMEM((tokens, channels), F32),
        pltpu.VMEM((tokens, channels), F32),
        *[slabs] * 6,
        pltpu.VMEM((channels, 2 * tokens), F32),
        pltpu.VMEM((2, PARTS, tokens, width), BF16),
        pltpu.VMEM((2, PARTS, tokens, width), BF16),
        pltpu.VMEM((PARTS, tokens, width), BF16),
        pltpu.VMEM((PARTS, tokens, width), BF16),
        pltpu.SemaphoreType.DMA((16,)),
        pltpu.SemaphoreType.DMA((3,)),
        pltpu.SemaphoreType.DMA((3,)),
        pltpu.SemaphoreType.DMA((3,)),
        pltpu.SemaphoreType.DMA((3,)),
        pltpu.SemaphoreType.DMA((2, PARTS)),
        pltpu.SemaphoreType.DMA((2, PARTS)),
        pltpu.SemaphoreType.DMA((PARTS,)),
        pltpu.SemaphoreType.DMA((PARTS,)),
    ]
    return pl.pallas_call(
        functools.partial(kernel, n),
        out_shape=jax.ShapeDtypeStruct((tokens, columns), BF16),
        in_specs=[hbm] * 13,
        out_specs=pl.BlockSpec(memory_space=pltpu.VMEM),
        scratch_shapes=scratch,
        compiler_params=pltpu.CompilerParams(
            collective_id=0, has_side_effects=True, vmem_limit_bytes=48 * 1024 * 1024
        ),
    )(
        q_stream,
        k_stream,
        v_stream,
        short_taps,
        long_filter,
        skip_gain.reshape(1, channels),
        out_weight,
        *tables,
    )


def solution(mesh):
    in_specs = (
        P("seq", "chan"),
        P("seq", "chan"),
        P("seq", "chan"),
        P(None, None, "chan"),
        P("seq", "chan"),
        P("chan"),
        P("chan", None),
    )
    return jax.shard_map(
        functools.partial(body, mesh.shape["seq"]),
        mesh=mesh,
        in_specs=in_specs,
        out_specs=P("seq", "chan"),
        check_vma=False,
    )
```

```python
import functools
import math

import jax
import jax.numpy as jnp
import ml_dtypes
import numpy as np
from jax import lax
from jax.experimental import pallas as pl
from jax.experimental.pallas import tpu as pltpu
from jax.sharding import PartitionSpec as P

MESH = pl.DeviceIdType.MESH
F32 = jnp.float32
BF16 = jnp.bfloat16
EDGE = 8
PARTS = 4
DEPTH = 8


def transform_tables(blocks, tokens):
    length = blocks * tokens
    frequency = np.arange(blocks) + 0.25
    outer_angle = 2 * math.pi * np.outer(frequency, np.arange(blocks)) / blocks
    outer = np.concatenate([np.cos(outer_angle), np.sin(outer_angle)])
    turn = 2 * math.pi * np.outer(frequency, np.arange(tokens)) / length
    inner_angle = 2 * math.pi * np.outer(np.arange(tokens), np.arange(tokens)) / tokens
    cosine, sine = np.cos(inner_angle), np.sin(inner_angle)
    inner = np.block([[cosine, sine], [-sine, cosine]])
    back = np.block([[cosine, -sine], [sine, cosine]]) / length
    matrices = [table.astype(ml_dtypes.bfloat16) for table in (outer, outer.T.copy(), inner, back)]
    return (*matrices, np.cos(turn).astype(np.float32), np.sin(turn).astype(np.float32))


def dot(a, b):
    return jnp.dot(a, b, preferred_element_type=F32)


def kernel(
    n,
    q_hbm,
    k_hbm,
    v_hbm,
    taps_hbm,
    filter_hbm,
    skip_hbm,
    weight_hbm,
    first_hbm,
    last_hbm,
    inner_hbm,
    back_hbm,
    cos_hbm,
    sin_hbm,
    out_ref,
    streams,
    taps,
    filt,
    skip,
    weight,
    first,
    last,
    inner,
    back,
    cosine,
    sine,
    halo_out,
    halo_in,
    tail,
    padded,
    product,
    q_short,
    skipped,
    send_h,
    send_p,
    send_y,
    recv_h,
    recv_p,
    recv_y,
    response,
    flat,
    send_core,
    recv_core,
    send_cross,
    recv_cross,
    load_sem,
    halo_send,
    halo_recv,
    all_send,
    all_recv,
    core_send,
    core_recv,
    cross_send,
    cross_recv,
):
    me, chan = lax.axis_index("seq"), lax.axis_index("chan")
    core, high = lax.rem(chan, 2), lax.div(chan, 2)
    other_core = high * 2 + 1 - core
    other_high = (1 - high) * 2 + core
    tokens, channels = filt.shape
    group = channels // n
    columns = weight.shape[2]

    def block_of(y_high, y_core):
        return weight_hbm.at[:, pl.ds(pl.multiple_of((y_high * 2 + y_core) * columns, columns), columns)]

    pairs = [
        (k_hbm, streams.at[1]),
        (v_hbm, streams.at[2]),
        (taps_hbm, taps),
        (filter_hbm, filt),
        (q_hbm, streams.at[0]),
        (skip_hbm, skip),
        (first_hbm, first),
        (cos_hbm, cosine),
        (sin_hbm, sine),
        (inner_hbm, inner),
        (back_hbm, back),
        (last_hbm, last),
        (block_of(1 - high, 1 - core), weight.at[0]),
        (block_of(1 - high, core), weight.at[1]),
        (block_of(high, 1 - core), weight.at[2]),
        (block_of(high, core), weight.at[3]),
    ]
    loads = [pltpu.make_async_copy(src, dst, load_sem.at[i]) for i, (src, dst) in enumerate(pairs)]
    for load in loads[:6]:
        load.start()

    barrier = pltpu.get_barrier_semaphore()

    @pl.loop(1, n)
    def _(d):
        pl.semaphore_signal(barrier, inc=1, device_id=(lax.rem(me + d, n), chan), device_id_type=MESH)

    pl.semaphore_signal(barrier, inc=1, device_id=(me, other_core), device_id_type=MESH)
    pl.semaphore_signal(barrier, inc=1, device_id=(me, other_high), device_id_type=MESH)
    for load in loads[6:12]:
        load.start()

    def exchange(source, target, index):
        def send(peer):
            pltpu.make_async_remote_copy(
                src_ref=source.at[peer],
                dst_ref=target.at[me],
                send_sem=all_send.at[index],
                recv_sem=all_recv.at[index],
                device_id=(peer, chan),
                device_id_type=MESH,
            ).start()

        place, depth = lax.div(me, DEPTH), lax.rem(me, DEPTH)
        across, pair = lax.div(place, 2), lax.rem(place, 2)
        for step_across, step_pair in ((2, 1), (2, 0), (1, 1), (3, 1), (1, 0), (3, 0), (0, 1), (0, 0)):
            line = (lax.rem(across + step_across, n // DEPTH // 2) * 2 + lax.rem(pair + step_pair, 2)) * DEPTH

            @pl.loop(0, DEPTH if step_across + step_pair else DEPTH - 1)
            def _(i):
                far = DEPTH // 2 - lax.div(i + 1, 2)
                step = jnp.where(lax.rem(i, 2) == 1, far, DEPTH - far)
                send(line + lax.rem(depth + step, DEPTH))

        target[me] = source[me]

    def arrived(buffer, index):
        part = buffer.at[pl.ds(0, n - 1)]
        pltpu.make_async_copy(part, part, all_recv.at[index]).wait()

    def left(buffer, index):
        part = buffer.at[pl.ds(0, n - 1)]
        pltpu.make_async_copy(part, part, all_send.at[index]).wait()

    def to_channels(value, buffer):
        per = tokens // group
        for i in range(channels // tokens):
            turned = value[:, i * tokens : (i + 1) * tokens].T
            buffer[i * per : (i + 1) * per] = turned.reshape(per, group, tokens).astype(BF16)

    edge = EDGE

    def short(i, rows):
        total = taps[i, 0:1] * padded[i, edge : edge + rows]
        for lag in range(1, taps.shape[1]):
            total += taps[i, lag : lag + 1] * padded[i, edge - lag : edge - lag + rows]
        return total

    def fill(i):
        padded[i, 0:edge] = jnp.zeros((edge, channels), F32)
        padded[i, edge : edge + tokens] = streams[i].astype(F32)

    for load in loads[0:3]:
        load.wait()
    fill(1)
    fill(2)
    product[...] = short(1, tokens) * short(2, tokens)
    to_channels(product[...], send_p)
    loads[3].wait()
    to_channels(filt[...], send_h)
    loads[4].wait()
    fill(0)

    rim = taps.shape[1] - 1
    tail[...] = jnp.zeros(tail.shape, F32)
    for i in range(3):
        tail[i * rim : (i + 1) * rim] = padded[i, edge + tokens - rim : edge + tokens]
    halo_out[...] = tail[...].astype(BF16)

    pl.semaphore_wait(barrier, n + 1)
    rims = pltpu.make_async_remote_copy(
        src_ref=halo_out,
        dst_ref=halo_in,
        send_sem=halo_send,
        recv_sem=halo_recv,
        device_id=(lax.rem(me + 1, n), chan),
        device_id_type=MESH,
    )
    rims.start()
    exchange(send_h, recv_h, 0)

    inside = jnp.where(me > 0, 1.0, 0.0).astype(F32)

    rims.wait_recv()
    tail[...] = halo_in[...].astype(F32) * inside
    for i in range(3):
        padded[i, edge - rim : edge] = tail[i * rim : (i + 1) * rim]
    head = short(1, edge) * short(2, edge)
    product[0:edge] = head
    for i in range(channels // tokens):
        per = tokens // group
        turned = head[:, i * tokens : (i + 1) * tokens].T.reshape(per, group, edge).astype(BF16)
        send_p[i * per : (i + 1) * per, :, 0:edge] = turned
    exchange(send_p, recv_p, 1)
    for load in loads[12:]:
        load.start()
    loads[5].wait()
    skipped[...] = skip[...] * product[...]
    q_short[...] = short(0, tokens)

    for load in loads[6:12]:
        load.wait()

    def forward(buffer):
        flat[...] = buffer[...].astype(F32).reshape(channels, tokens)
        signal = [flat[pl.ds(c, n, stride=group)].astype(BF16) for c in range(group)]
        stage = dot(first[...], jnp.concatenate(signal, axis=1))
        turned = []
        for c in range(group):
            real, imag = stage[:n, c * tokens : (c + 1) * tokens], stage[n:, c * tokens : (c + 1) * tokens]
            pair = [real * cosine[...] - imag * sine[...], real * sine[...] + imag * cosine[...]]
            turned.append(jnp.concatenate(pair, axis=1).astype(BF16))
        return dot(jnp.concatenate(turned, axis=0), inner[...])

    arrived(recv_h, 0)
    response[...] = forward(recv_h)
    arrived(recv_p, 1)
    spectrum = forward(recv_p)
    p_real, p_imag = spectrum[:, :tokens], spectrum[:, tokens:]
    h_real, h_imag = response[:, :tokens], response[:, tokens:]
    filtered = [p_real * h_real - p_imag * h_imag, p_real * h_imag + p_imag * h_real]
    mixed = dot(jnp.concatenate(filtered, axis=1).astype(BF16), back[...])
    turned = []
    for c in range(group):
        real, imag = mixed[c * n : (c + 1) * n, :tokens], mixed[c * n : (c + 1) * n, tokens:]
        pair = [real * cosine[...] + imag * sine[...], imag * cosine[...] - real * sine[...]]
        turned.append(jnp.concatenate(pair, axis=0).astype(BF16))
    convolved = dot(last[...], jnp.concatenate(turned, axis=1))
    for c in range(group):
        flat[pl.ds(c, n, stride=group)] = convolved[:, c * tokens : (c + 1) * tokens]
    send_y[...] = flat[...].reshape(n, group, tokens).astype(BF16)
    exchange(send_y, recv_y, 2)
    arrived(recv_y, 2)

    long_part = recv_y[...].astype(F32).reshape(channels, tokens)
    long_part = jnp.concatenate([long_part[i * tokens : (i + 1) * tokens].T for i in range(channels // tokens)], axis=1)
    gated = (q_short[...] * (long_part + skipped[...])).astype(BF16)

    width = columns // PARTS

    def project(i, part):
        return dot(gated, weight[i, :, part * width : (part + 1) * width])

    def core_copy(half, part):
        return pltpu.make_async_remote_copy(
            src_ref=send_core.at[half, part],
            dst_ref=recv_core.at[half, part],
            send_sem=core_send.at[half, part],
            recv_sem=core_recv.at[half, part],
            device_id=(me, other_core),
            device_id_type=MESH,
        )

    def cross_copy(part):
        return pltpu.make_async_remote_copy(
            src_ref=send_cross.at[part],
            dst_ref=recv_cross.at[part],
            send_sem=cross_send.at[part],
            recv_sem=cross_recv.at[part],
            device_id=(me, other_high),
            device_id_type=MESH,
        )

    for load in loads[12:]:
        load.wait()
    kept = []
    for part in range(PARTS):
        send_core[0, part] = project(0, part).astype(BF16)
        core_copy(0, part).start()
        kept.append(project(1, part))
    for part in range(PARTS):
        core_copy(0, part).wait_recv()
        send_cross[part] = (kept[part] + recv_core[0, part].astype(F32)).astype(BF16)
        cross_copy(part).start()
    for part in range(PARTS):
        send_core[1, part] = project(2, part).astype(BF16)
        core_copy(1, part).start()
    for part in range(PARTS):
        mine = project(3, part)
        core_copy(1, part).wait_recv()
        mine = mine + recv_core[1, part].astype(F32)
        cross_copy(part).wait_recv()
        out_ref[:, part * width : (part + 1) * width] = (mine + recv_cross[part].astype(F32)).astype(BF16)

    rims.wait_send()
    left(send_h, 0)
    left(send_p, 1)
    left(send_y, 2)
    for part in range(PARTS):
        core_copy(0, part).wait_send()
        core_copy(1, part).wait_send()
        cross_copy(part).wait_send()


def body(n, q_stream, k_stream, v_stream, short_taps, long_filter, skip_gain, out_weight):
    tokens, channels = long_filter.shape
    rows, features = out_weight.shape
    columns = features // lax.axis_size("chan")
    group = channels // n
    tables = transform_tables(n, tokens)
    hbm = pl.BlockSpec(memory_space=pltpu.HBM)
    operands = [
        q_stream,
        k_stream,
        v_stream,
        short_taps,
        long_filter,
        skip_gain.reshape(1, channels),
        out_weight,
        *tables,
    ]
    width = columns // PARTS
    slabs = pltpu.VMEM((n, group, tokens), BF16)
    scratch = [
        pltpu.VMEM((3, tokens, channels), BF16),
        pltpu.VMEM(short_taps.shape, F32),
        pltpu.VMEM((tokens, channels), F32),
        pltpu.VMEM((1, channels), F32),
        pltpu.VMEM((4, rows, columns), BF16),
        *[pltpu.VMEM(table.shape, table.dtype) for table in tables],
        pltpu.VMEM((EDGE, channels), BF16),
        pltpu.VMEM((EDGE, channels), BF16),
        pltpu.VMEM((EDGE, channels), F32),
        pltpu.VMEM((3, EDGE + tokens, channels), F32),
        pltpu.VMEM((tokens, channels), F32),
        pltpu.VMEM((tokens, channels), F32),
        pltpu.VMEM((tokens, channels), F32),
        *[slabs] * 6,
        pltpu.VMEM((channels, 2 * tokens), F32),
        pltpu.VMEM((channels, tokens), F32),
        pltpu.VMEM((2, PARTS, tokens, width), BF16),
        pltpu.VMEM((2, PARTS, tokens, width), BF16),
        pltpu.VMEM((PARTS, tokens, width), BF16),
        pltpu.VMEM((PARTS, tokens, width), BF16),
        pltpu.SemaphoreType.DMA((16,)),
        pltpu.SemaphoreType.DMA,
        pltpu.SemaphoreType.DMA,
        pltpu.SemaphoreType.DMA((3,)),
        pltpu.SemaphoreType.DMA((3,)),
        pltpu.SemaphoreType.DMA((2, PARTS)),
        pltpu.SemaphoreType.DMA((2, PARTS)),
        pltpu.SemaphoreType.DMA((PARTS,)),
        pltpu.SemaphoreType.DMA((PARTS,)),
    ]
    return pl.pallas_call(
        functools.partial(kernel, n),
        out_shape=pltpu.VMEM((tokens, columns), BF16),
        in_specs=[hbm] * 13,
        out_specs=pl.BlockSpec(memory_space=pltpu.VMEM),
        scratch_shapes=scratch,
        compiler_params=pltpu.CompilerParams(
            collective_id=0, has_side_effects=True, vmem_limit_bytes=40 * 1024 * 1024
        ),
    )(*[pltpu.with_memory_space_constraint(jnp.asarray(each), pltpu.HBM) for each in operands])


def solution(mesh):
    in_specs = (
        P("seq", "chan"),
        P("seq", "chan"),
        P("seq", "chan"),
        P(None, None, "chan"),
        P("seq", "chan"),
        P("chan"),
        P("chan", None),
    )
    return jax.shard_map(
        functools.partial(body, mesh.shape["seq"]),
        mesh=mesh,
        in_specs=in_specs,
        out_specs=P("seq", "chan"),
        check_vma=False,
    )
```

```python
import functools
import math

import jax
import jax.numpy as jnp
import ml_dtypes
import numpy as np
from jax import lax
from jax.experimental import pallas as pl
from jax.experimental.pallas import tpu as pltpu
from jax.sharding import PartitionSpec as P

MESH = pl.DeviceIdType.MESH
F32 = jnp.float32
BF16 = jnp.bfloat16
EDGE = 8
PARTS = 2
DEPTH = 8


def transform_tables(blocks, tokens):
    length = blocks * tokens
    frequency = np.arange(blocks) + 0.25
    outer_angle = 2 * math.pi * np.outer(frequency, np.arange(blocks)) / blocks
    outer = np.concatenate([np.cos(outer_angle), np.sin(outer_angle)])
    turn = 2 * math.pi * np.outer(frequency, np.arange(tokens)) / length
    inner_angle = 2 * math.pi * np.outer(np.arange(tokens), np.arange(tokens)) / tokens
    cosine, sine = np.cos(inner_angle), np.sin(inner_angle)
    inner = np.block([[cosine, sine], [-sine, cosine]])
    back = np.block([[cosine, -sine], [sine, cosine]]) / length
    matrices = [table.astype(ml_dtypes.bfloat16) for table in (outer, outer.T.copy(), inner, back)]
    return (*matrices, np.cos(turn).astype(np.float32), np.sin(turn).astype(np.float32))


def dot(a, b):
    return jnp.dot(a, b, preferred_element_type=F32)


def kernel(
    n,
    q_hbm,
    k_hbm,
    v_hbm,
    taps_hbm,
    filter_hbm,
    skip_hbm,
    weight_hbm,
    first_hbm,
    last_hbm,
    inner_hbm,
    back_hbm,
    cos_hbm,
    sin_hbm,
    out_ref,
    streams,
    taps,
    filt,
    skip,
    cross_weight,
    own_weight,
    first,
    last,
    inner,
    back,
    cosine,
    sine,
    halo_out,
    halo_in,
    tail,
    padded,
    product,
    q_short,
    skipped,
    send_h,
    send_p,
    send_y,
    recv_h,
    recv_p,
    recv_y,
    response,
    flat,
    gated,
    mine,
    own,
    send_cross,
    recv_cross,
    load_sem,
    halo_send,
    halo_recv,
    all_send,
    all_recv,
    weight_send,
    weight_recv,
    gated_send,
    gated_recv,
    cross_send,
    cross_recv,
):
    me, chan = lax.axis_index("seq"), lax.axis_index("chan")
    core, high = lax.rem(chan, 2), lax.div(chan, 2)
    other_core = high * 2 + 1 - core
    across = ((1 - high) * 2 + 1, (1 - high) * 2)
    tokens, channels = filt.shape
    group = channels // n
    columns = own_weight.shape[2]

    half = columns // 2

    def weight_part(feature_block, start, width):
        return weight_hbm.at[:, pl.ds(pl.multiple_of(feature_block * columns + start, half), width)]

    def parts_for(which):
        return [
            weight_part((1 - high) * 2 + 1, which * half, half),
            weight_part((1 - high) * 2, which * half, half),
            weight_part(high * 2 + which, 0, columns),
        ]

    def weight_slots(row):
        return [cross_weight.at[0, row], cross_weight.at[1, row], own_weight.at[row]]

    pairs = [
        (k_hbm, streams.at[1]),
        (v_hbm, streams.at[2]),
        (taps_hbm, taps),
        (filter_hbm, filt),
        (q_hbm, streams.at[0]),
        (skip_hbm, skip),
        (first_hbm, first),
        (cos_hbm, cosine),
        (sin_hbm, sine),
        (inner_hbm, inner),
        (back_hbm, back),
        (last_hbm, last),
        *zip(parts_for(core), weight_slots(0)),
    ]
    loads = [pltpu.make_async_copy(src, dst, load_sem.at[i]) for i, (src, dst) in enumerate(pairs)]
    for load in loads[:6]:
        load.start()

    barrier = pltpu.get_barrier_semaphore()

    @pl.loop(1, n)
    def _(d):
        pl.semaphore_signal(barrier, inc=1, device_id=(lax.rem(me + d, n), chan), device_id_type=MESH)

    for neighbour in (other_core, *across):
        pl.semaphore_signal(barrier, inc=1, device_id=(me, neighbour), device_id_type=MESH)
    for load in loads[6:12]:
        load.start()

    def exchange(source, target, index):
        def send(peer):
            pltpu.make_async_remote_copy(
                src_ref=source.at[peer],
                dst_ref=target.at[me],
                send_sem=all_send.at[index],
                recv_sem=all_recv.at[index],
                device_id=(peer, chan),
                device_id_type=MESH,
            ).start()

        place, depth = lax.div(me, DEPTH), lax.rem(me, DEPTH)
        row, pair = lax.div(place, 2), lax.rem(place, 2)
        for step_across, step_pair in ((2, 1), (2, 0), (1, 1), (3, 1), (1, 0), (3, 0), (0, 1), (0, 0)):
            line = (lax.rem(row + step_across, n // DEPTH // 2) * 2 + lax.rem(pair + step_pair, 2)) * DEPTH

            @pl.loop(0, DEPTH if step_across + step_pair else DEPTH - 1)
            def _(i):
                far = DEPTH // 2 - lax.div(i + 1, 2)
                step = jnp.where(lax.rem(i, 2) == 1, far, DEPTH - far)
                send(line + lax.rem(depth + step, DEPTH))

        target[me] = source[me]

    def arrived(buffer, index):
        part = buffer.at[pl.ds(0, n - 1)]
        pltpu.make_async_copy(part, part, all_recv.at[index]).wait()

    def left(buffer, index):
        part = buffer.at[pl.ds(0, n - 1)]
        pltpu.make_async_copy(part, part, all_send.at[index]).wait()

    def to_channels(value, buffer):
        per = tokens // group
        for i in range(channels // tokens):
            turned = value[:, i * tokens : (i + 1) * tokens].T
            buffer[i * per : (i + 1) * per] = turned.reshape(per, group, tokens).astype(BF16)

    edge = EDGE

    def short(i, rows):
        total = taps[i, 0:1] * padded[i, edge : edge + rows]
        for lag in range(1, taps.shape[1]):
            total += taps[i, lag : lag + 1] * padded[i, edge - lag : edge - lag + rows]
        return total

    def fill(i):
        padded[i, 0:edge] = jnp.zeros((edge, channels), F32)
        padded[i, edge : edge + tokens] = streams[i].astype(F32)

    for load in loads[0:3]:
        load.wait()
    fill(1)
    fill(2)
    product[...] = short(1, tokens) * short(2, tokens)
    to_channels(product[...], send_p)
    loads[3].wait()
    to_channels(filt[...], send_h)
    loads[4].wait()
    fill(0)

    rim = taps.shape[1] - 1
    tail[...] = jnp.zeros(tail.shape, F32)
    for i in range(3):
        tail[i * rim : (i + 1) * rim] = padded[i, edge + tokens - rim : edge + tokens]
    halo_out[...] = tail[...].astype(BF16)

    pl.semaphore_wait(barrier, n + 2)
    rims = pltpu.make_async_remote_copy(
        src_ref=halo_out,
        dst_ref=halo_in,
        send_sem=halo_send,
        recv_sem=halo_recv,
        device_id=(lax.rem(me + 1, n), chan),
        device_id_type=MESH,
    )
    rims.start()
    exchange(send_h, recv_h, 0)

    inside = jnp.where(me > 0, 1.0, 0.0).astype(F32)

    rims.wait_recv()
    tail[...] = halo_in[...].astype(F32) * inside
    for i in range(3):
        padded[i, edge - rim : edge] = tail[i * rim : (i + 1) * rim]
    head = short(1, edge) * short(2, edge)
    product[0:edge] = head
    for i in range(channels // tokens):
        per = tokens // group
        turned = head[:, i * tokens : (i + 1) * tokens].T.reshape(per, group, edge).astype(BF16)
        send_p[i * per : (i + 1) * per, :, 0:edge] = turned
    exchange(send_p, recv_p, 1)
    for load in loads[12:]:
        load.start()
    handed = []
    for i, (src, dst) in enumerate(zip(parts_for(1 - core), weight_slots(1))):
        handed.append(
            pltpu.make_async_remote_copy(
                src_ref=src,
                dst_ref=dst,
                send_sem=weight_send.at[i],
                recv_sem=weight_recv.at[i],
                device_id=(me, other_core),
                device_id_type=MESH,
            )
        )
        handed[-1].start()
    loads[5].wait()
    skipped[...] = skip[...] * product[...]
    q_short[...] = short(0, tokens)

    for load in loads[6:12]:
        load.wait()

    def forward(buffer):
        flat[...] = buffer[...].astype(F32).reshape(channels, tokens)
        signal = [flat[pl.ds(c, n, stride=group)].astype(BF16) for c in range(group)]
        stage = dot(first[...], jnp.concatenate(signal, axis=1))
        turned = []
        for c in range(group):
            real, imag = stage[:n, c * tokens : (c + 1) * tokens], stage[n:, c * tokens : (c + 1) * tokens]
            pair = [real * cosine[...] - imag * sine[...], real * sine[...] + imag * cosine[...]]
            turned.append(jnp.concatenate(pair, axis=1).astype(BF16))
        return dot(jnp.concatenate(turned, axis=0), inner[...])

    arrived(recv_h, 0)
    response[...] = forward(recv_h)
    arrived(recv_p, 1)
    spectrum = forward(recv_p)
    p_real, p_imag = spectrum[:, :tokens], spectrum[:, tokens:]
    h_real, h_imag = response[:, :tokens], response[:, tokens:]
    filtered = [p_real * h_real - p_imag * h_imag, p_real * h_imag + p_imag * h_real]
    mixed = dot(jnp.concatenate(filtered, axis=1).astype(BF16), back[...])
    turned = []
    for c in range(group):
        real, imag = mixed[c * n : (c + 1) * n, :tokens], mixed[c * n : (c + 1) * n, tokens:]
        pair = [real * cosine[...] + imag * sine[...], imag * cosine[...] - real * sine[...]]
        turned.append(jnp.concatenate(pair, axis=0).astype(BF16))
    convolved = dot(last[...], jnp.concatenate(turned, axis=1))
    for c in range(group):
        flat[pl.ds(c, n, stride=group)] = convolved[:, c * tokens : (c + 1) * tokens]
    send_y[...] = flat[...].reshape(n, group, tokens).astype(BF16)
    exchange(send_y, recv_y, 2)
    arrived(recv_y, 2)

    long_part = recv_y[...].astype(F32).reshape(channels, tokens)
    long_part = jnp.concatenate([long_part[i * tokens : (i + 1) * tokens].T for i in range(channels // tokens)], axis=1)
    gated[0] = (q_short[...] * (long_part + skipped[...])).astype(BF16)
    swap = pltpu.make_async_remote_copy(
        src_ref=gated.at[0],
        dst_ref=gated.at[1],
        send_sem=gated_send,
        recv_sem=gated_recv,
        device_id=(me, other_core),
        device_id_type=MESH,
    )
    swap.start()

    width = half // PARTS

    def cross_copy(target, part):
        return pltpu.make_async_remote_copy(
            src_ref=send_cross.at[target, part],
            dst_ref=recv_cross.at[core, part],
            send_sem=cross_send.at[target, part],
            recv_sem=cross_recv.at[core, part],
            device_id=(me, across[target]),
            device_id_type=MESH,
        )

    def cross_arrived(source, part):
        pltpu.make_async_copy(recv_cross.at[source, part], recv_cross.at[source, part], cross_recv.at[source, part]).wait()

    steps = [(target, part) for target in range(2) for part in range(PARTS)]
    for load in loads[12:]:
        load.wait()

    def project(row, target, part):
        return dot(gated[row], cross_weight[target, row, :, part * width : (part + 1) * width])

    for target, part in steps:
        mine[target, part] = project(0, target, part)
    for copy in handed:
        copy.wait_recv()
    swap.wait_recv()
    for target, part in steps:
        send_cross[target, part] = (mine[target, part] + project(1, target, part)).astype(BF16)
        cross_copy(target, part).start()
    for part in range(2 * PARTS):
        span = slice(part * width, (part + 1) * width)
        own[:, span] = dot(gated[0], own_weight[0, :, span]) + dot(gated[1], own_weight[1, :, span])
    for part in range(PARTS):
        for source in range(2):
            span = slice(source * half + part * width, source * half + (part + 1) * width)
            cross_arrived(source, part)
            out_ref[:, span] = (own[:, span] + recv_cross[source, part].astype(F32)).astype(BF16)

    rims.wait_send()
    left(send_h, 0)
    left(send_p, 1)
    left(send_y, 2)
    swap.wait_send()
    for copy in handed:
        copy.wait_send()
    for target, part in steps:
        cross_copy(target, part).wait_send()


def body(n, q_stream, k_stream, v_stream, short_taps, long_filter, skip_gain, out_weight):
    tokens, channels = long_filter.shape
    rows, features = out_weight.shape
    columns = features // lax.axis_size("chan")
    group = channels // n
    tables = transform_tables(n, tokens)
    hbm = pl.BlockSpec(memory_space=pltpu.HBM)
    operands = [
        q_stream,
        k_stream,
        v_stream,
        short_taps,
        long_filter,
        skip_gain.reshape(1, channels),
        out_weight,
        *tables,
    ]
    width = columns // 2 // PARTS
    slabs = pltpu.VMEM((n, group, tokens), BF16)
    scratch = [
        pltpu.VMEM((3, tokens, channels), BF16),
        pltpu.VMEM(short_taps.shape, F32),
        pltpu.VMEM((tokens, channels), F32),
        pltpu.VMEM((1, channels), F32),
        pltpu.VMEM((2, 2, rows, columns // 2), BF16),
        pltpu.VMEM((2, rows, columns), BF16),
        *[pltpu.VMEM(table.shape, table.dtype) for table in tables],
        pltpu.VMEM((EDGE, channels), BF16),
        pltpu.VMEM((EDGE, channels), BF16),
        pltpu.VMEM((EDGE, channels), F32),
        pltpu.VMEM((3, EDGE + tokens, channels), F32),
        pltpu.VMEM((tokens, channels), F32),
        pltpu.VMEM((tokens, channels), F32),
        pltpu.VMEM((tokens, channels), F32),
        *[slabs] * 6,
        pltpu.VMEM((channels, 2 * tokens), F32),
        pltpu.VMEM((channels, tokens), F32),
        pltpu.VMEM((2, tokens, channels), BF16),
        pltpu.VMEM((2, PARTS, tokens, width), F32),
        pltpu.VMEM((tokens, columns), F32),
        pltpu.VMEM((2, PARTS, tokens, width), BF16),
        pltpu.VMEM((2, PARTS, tokens, width), BF16),
        pltpu.SemaphoreType.DMA((16,)),
        pltpu.SemaphoreType.DMA,
        pltpu.SemaphoreType.DMA,
        pltpu.SemaphoreType.DMA((3,)),
        pltpu.SemaphoreType.DMA((3,)),
        pltpu.SemaphoreType.DMA((3,)),
        pltpu.SemaphoreType.DMA((3,)),
        pltpu.SemaphoreType.DMA,
        pltpu.SemaphoreType.DMA,
        pltpu.SemaphoreType.DMA((2, PARTS)),
        pltpu.SemaphoreType.DMA((2, PARTS)),
    ]
    return pl.pallas_call(
        functools.partial(kernel, n),
        out_shape=pltpu.VMEM((tokens, columns), BF16),
        in_specs=[hbm] * 13,
        out_specs=pl.BlockSpec(memory_space=pltpu.VMEM),
        scratch_shapes=scratch,
        compiler_params=pltpu.CompilerParams(
            collective_id=0, has_side_effects=True, vmem_limit_bytes=40 * 1024 * 1024
        ),
    )(*[pltpu.with_memory_space_constraint(jnp.asarray(each), pltpu.HBM) for each in operands])


def solution(mesh):
    in_specs = (
        P("seq", "chan"),
        P("seq", "chan"),
        P("seq", "chan"),
        P(None, None, "chan"),
        P("seq", "chan"),
        P("chan"),
        P("chan", None),
    )
    return jax.shard_map(
        functools.partial(body, mesh.shape["seq"]),
        mesh=mesh,
        in_specs=in_specs,
        out_specs=P("seq", "chan"),
        check_vma=False,
    )
```

```python
import functools
import math

import jax
import jax.numpy as jnp
import ml_dtypes
import numpy as np
from jax import lax
from jax.experimental import pallas as pl
from jax.experimental.pallas import tpu as pltpu
from jax.sharding import PartitionSpec as P

MESH = pl.DeviceIdType.MESH
F32 = jnp.float32
BF16 = jnp.bfloat16
EDGE = 8
PARTS = 2
DEPTH = 8


def transform_tables(blocks, tokens):
    length = blocks * tokens
    frequency = np.arange(blocks) + 0.25
    outer_angle = 2 * math.pi * np.outer(frequency, np.arange(blocks)) / blocks
    outer = np.concatenate([np.cos(outer_angle), np.sin(outer_angle)])
    turn = 2 * math.pi * np.outer(frequency, np.arange(tokens)) / length
    inner_angle = 2 * math.pi * np.outer(np.arange(tokens), np.arange(tokens)) / tokens
    cosine, sine = np.cos(inner_angle), np.sin(inner_angle)
    inner = np.block([[cosine, sine], [-sine, cosine]])
    back = np.block([[cosine, -sine], [sine, cosine]]) / length
    matrices = [table.astype(ml_dtypes.bfloat16) for table in (outer, outer.T.copy(), inner, back)]
    return (*matrices, np.cos(turn).astype(np.float32), np.sin(turn).astype(np.float32))


def dot(a, b):
    return jnp.dot(a, b, preferred_element_type=F32)


def kernel(
    n,
    q_hbm,
    k_hbm,
    v_hbm,
    taps_hbm,
    filter_hbm,
    skip_hbm,
    weight_hbm,
    first_hbm,
    last_hbm,
    inner_hbm,
    back_hbm,
    cos_hbm,
    sin_hbm,
    out_ref,
    streams,
    taps,
    filt,
    skip,
    cross_weight,
    own_weight,
    first,
    last,
    inner,
    back,
    cosine,
    sine,
    halo_out,
    halo_in,
    tail,
    edge_out,
    edge_in,
    padded,
    product,
    q_short,
    skipped,
    send_h,
    send_p,
    send_y,
    recv_h,
    recv_p,
    recv_y,
    response,
    flat,
    gated,
    mine,
    own,
    send_cross,
    recv_cross,
    load_sem,
    halo_send,
    halo_recv,
    all_send,
    all_recv,
    weight_send,
    weight_recv,
    gated_send,
    gated_recv,
    cross_send,
    cross_recv,
    turn_sem,
):
    me, chan = lax.axis_index("seq"), lax.axis_index("chan")
    core, high = lax.rem(chan, 2), lax.div(chan, 2)
    other_core = high * 2 + 1 - core
    across = ((1 - high) * 2 + 1, (1 - high) * 2)
    tokens, channels = filt.shape
    group = channels // n
    columns = own_weight.shape[2]

    half = columns // 2

    def weight_part(feature_block, start, width):
        return weight_hbm.at[:, pl.ds(pl.multiple_of(feature_block * columns + start, half), width)]

    def parts_for(which):
        return [
            weight_part((1 - high) * 2 + 1, which * half, half),
            weight_part((1 - high) * 2, which * half, half),
            weight_part(high * 2 + which, 0, columns),
        ]

    def weight_slots(row):
        return [cross_weight.at[0, row], cross_weight.at[1, row], own_weight.at[row]]

    pairs = [
        (k_hbm, streams.at[1]),
        (v_hbm, streams.at[2]),
        (taps_hbm, taps),
        (filter_hbm, filt),
        (q_hbm, streams.at[0]),
        (skip_hbm, skip),
        (first_hbm, first),
        (cos_hbm, cosine),
        (sin_hbm, sine),
        (inner_hbm, inner),
        (back_hbm, back),
        (last_hbm, last),
        *zip(parts_for(core), weight_slots(0)),
    ]
    loads = [pltpu.make_async_copy(src, dst, load_sem.at[i]) for i, (src, dst) in enumerate(pairs)]
    for load in loads[:6]:
        load.start()

    barrier = pltpu.get_barrier_semaphore()

    @pl.loop(1, n)
    def _(d):
        pl.semaphore_signal(barrier, inc=1, device_id=(lax.rem(me + d, n), chan), device_id_type=MESH)

    for neighbour in (other_core, *across):
        pl.semaphore_signal(barrier, inc=1, device_id=(me, neighbour), device_id_type=MESH)
    for load in loads[6:12]:
        load.start()

    def exchange(*routes):
        def send(peer):
            for source, target, index in routes:
                pltpu.make_async_remote_copy(
                    src_ref=source(peer),
                    dst_ref=target(me),
                    send_sem=all_send.at[index],
                    recv_sem=all_recv.at[index],
                    device_id=(peer, chan),
                    device_id_type=MESH,
                ).start()

        place, depth = lax.div(me, DEPTH), lax.rem(me, DEPTH)
        row, pair = lax.div(place, 2), lax.rem(place, 2)
        for step_row, step_pair in ((2, 1), (2, 0), (1, 1), (3, 1), (1, 0), (3, 0), (0, 1), (0, 0)):
            line = (lax.rem(row + step_row, n // DEPTH // 2) * 2 + lax.rem(pair + step_pair, 2)) * DEPTH

            @pl.loop(0, DEPTH if step_row + step_pair else DEPTH - 1)
            def _(i):
                far = DEPTH // 2 - lax.div(i + 1, 2)
                step = jnp.where(lax.rem(i, 2) == 1, far, DEPTH - far)
                send(line + lax.rem(depth + step, DEPTH))

    def slabs(source, target, index):
        return (lambda peer: source.at[peer], lambda own_place: target.at[own_place], index)

    edges = (
        lambda peer: edge_out.at[pl.ds(peer, 1)],
        lambda own_place: edge_in.at[pl.ds(edge + own_place, 1)],
        3,
    )

    def arrived(buffer, index):
        part = buffer.at[pl.ds(0, n - 1)]
        pltpu.make_async_copy(part, part, all_recv.at[index]).wait()

    def left(buffer, index):
        part = buffer.at[pl.ds(0, n - 1)]
        pltpu.make_async_copy(part, part, all_send.at[index]).wait()

    def to_channels(value, buffer):
        per = tokens // group
        for i in range(channels // tokens):
            turned = value[:, i * tokens : (i + 1) * tokens].T
            buffer[i * per : (i + 1) * per] = turned.reshape(per, group, tokens).astype(BF16)

    edge = EDGE

    def short(i, first_row, rows):
        start = edge + first_row
        total = taps[i, 0:1] * padded[i, start : start + rows]
        for lag in range(1, taps.shape[1]):
            total += taps[i, lag : lag + 1] * padded[i, start - lag : start - lag + rows]
        return total

    def fill(i):
        padded[i, 0:edge] = jnp.zeros((edge, channels), F32)
        padded[i, edge : edge + tokens] = streams[i].astype(F32)
        padded[i, edge + tokens :] = jnp.zeros((edge, channels), F32)

    for load in loads[0:3]:
        load.wait()
    fill(1)
    fill(2)
    k_short, v_short = short(1, 0, tokens), short(2, 0, tokens)
    product[...] = k_short * v_short
    to_channels(product[...], send_p)
    rim = taps.shape[1] - 1
    for i, value in enumerate((k_short, v_short, short(1, tokens, edge), short(2, tokens, edge))):
        tail[i * rim : (i + 1) * rim] = value[:rim]
    for i in range(channels // tokens):
        flat[i * tokens : (i + 1) * tokens, 0:edge] = tail[:, i * tokens : (i + 1) * tokens].T
    pieces = [flat[pl.ds(c, n, stride=group)][:, 0:edge] for c in range(group)]
    edge_out[:, 0 : group * edge] = jnp.concatenate(pieces, axis=1)
    edge_out[:, group * edge :] = jnp.zeros((n, tokens - group * edge), F32)
    edge_in[0:edge] = jnp.zeros((edge, tokens), F32)
    loads[3].wait()
    to_channels(filt[...], send_h)
    loads[4].wait()
    fill(0)

    tail[...] = jnp.zeros(tail.shape, F32)
    for i in range(3):
        tail[i * rim : (i + 1) * rim] = padded[i, edge + tokens - rim : edge + tokens]
    halo_out[...] = tail[...].astype(BF16)

    pl.semaphore_wait(barrier, n + 2)
    rims = pltpu.make_async_remote_copy(
        src_ref=halo_out,
        dst_ref=halo_in,
        send_sem=halo_send,
        recv_sem=halo_recv,
        device_id=(lax.rem(me + 1, n), chan),
        device_id_type=MESH,
    )
    exchange(slabs(send_h, recv_h, 0))

    @pl.when(core == 1)
    def _():
        pl.semaphore_wait(turn_sem, 1)

    exchange(slabs(send_p, recv_p, 1), edges)

    @pl.when(core == 0)
    def _():
        left(send_h, 0)
        pl.semaphore_signal(turn_sem, inc=1, device_id=(me, other_core), device_id_type=MESH)

    rims.start()
    recv_h[me] = send_h[me]
    recv_p[me] = send_p[me]
    edge_in[pl.ds(edge + me, 1)] = edge_out[pl.ds(me, 1)]
    for load in loads[12:]:
        load.start()
    handed = []
    for i, (src, dst) in enumerate(zip(parts_for(1 - core), weight_slots(1))):
        handed.append(
            pltpu.make_async_remote_copy(
                src_ref=src,
                dst_ref=dst,
                send_sem=weight_send.at[i],
                recv_sem=weight_recv.at[i],
                device_id=(me, other_core),
                device_id_type=MESH,
            )
        )
        handed[-1].start()
    for load in loads[6:12]:
        load.wait()

    def forward(buffer, heads=None):
        flat[...] = buffer[...].astype(F32).reshape(channels, tokens)
        signal = [flat[pl.ds(c, n, stride=group)] for c in range(group)]
        if heads is not None:
            first_lanes = lax.broadcasted_iota(jnp.int32, (n, tokens), 1) < rim
            moved = [pltpu.roll(heads, (tokens - c * edge) % tokens, axis=1) for c in range(group)]
            signal = [jnp.where(first_lanes, new, old) for new, old in zip(moved, signal)]
        signal = [value.astype(BF16) for value in signal]
        stage = dot(first[...], jnp.concatenate(signal, axis=1))
        turned = []
        for c in range(group):
            real, imag = stage[:n, c * tokens : (c + 1) * tokens], stage[n:, c * tokens : (c + 1) * tokens]
            pair = [real * cosine[...] - imag * sine[...], real * sine[...] + imag * cosine[...]]
            turned.append(jnp.concatenate(pair, axis=1).astype(BF16))
        return dot(jnp.concatenate(turned, axis=0), inner[...])

    arrived(recv_h, 0)
    response[...] = forward(recv_h)
    arrived(recv_p, 1)
    pltpu.make_async_copy(edge_in.at[pl.ds(0, n - 1)], edge_in.at[pl.ds(0, n - 1)], all_recv.at[3]).wait()
    before = pltpu.roll(edge_in[edge - 1 : edge - 1 + n], tokens - 2 * rim, axis=1)
    completed = edge_in[edge : edge + n] + before
    heads = completed * pltpu.roll(completed, tokens - rim, axis=1)
    spectrum = forward(recv_p, heads)
    p_real, p_imag = spectrum[:, :tokens], spectrum[:, tokens:]
    h_real, h_imag = response[:, :tokens], response[:, tokens:]
    filtered = [p_real * h_real - p_imag * h_imag, p_real * h_imag + p_imag * h_real]
    mixed = dot(jnp.concatenate(filtered, axis=1).astype(BF16), back[...])
    turned = []
    for c in range(group):
        real, imag = mixed[c * n : (c + 1) * n, :tokens], mixed[c * n : (c + 1) * n, tokens:]
        pair = [real * cosine[...] + imag * sine[...], imag * cosine[...] - real * sine[...]]
        turned.append(jnp.concatenate(pair, axis=0).astype(BF16))
    convolved = dot(last[...], jnp.concatenate(turned, axis=1))
    for c in range(group):
        flat[pl.ds(c, n, stride=group)] = convolved[:, c * tokens : (c + 1) * tokens]
    send_y[...] = flat[...].reshape(n, group, tokens).astype(BF16)
    exchange(slabs(send_y, recv_y, 2))
    recv_y[me] = send_y[me]
    loads[5].wait()
    rims.wait_recv()
    inside = jnp.where(me > 0, 1.0, 0.0).astype(F32)
    tail[...] = halo_in[...].astype(F32) * inside
    for i in range(3):
        padded[i, edge - rim : edge] = tail[i * rim : (i + 1) * rim]
    product[0:edge] = short(1, 0, edge) * short(2, 0, edge)
    skipped[...] = skip[...] * product[...]
    q_short[...] = short(0, 0, tokens)
    arrived(recv_y, 2)

    long_part = recv_y[...].astype(F32).reshape(channels, tokens)
    long_part = jnp.concatenate([long_part[i * tokens : (i + 1) * tokens].T for i in range(channels // tokens)], axis=1)
    gated[0] = (q_short[...] * (long_part + skipped[...])).astype(BF16)
    swap = pltpu.make_async_remote_copy(
        src_ref=gated.at[0],
        dst_ref=gated.at[1],
        send_sem=gated_send,
        recv_sem=gated_recv,
        device_id=(me, other_core),
        device_id_type=MESH,
    )
    swap.start()

    width = half // PARTS

    def cross_copy(target, part):
        return pltpu.make_async_remote_copy(
            src_ref=send_cross.at[target, part],
            dst_ref=recv_cross.at[core, part],
            send_sem=cross_send.at[target, part],
            recv_sem=cross_recv.at[core, part],
            device_id=(me, across[target]),
            device_id_type=MESH,
        )

    def cross_arrived(source, part):
        pltpu.make_async_copy(recv_cross.at[source, part], recv_cross.at[source, part], cross_recv.at[source, part]).wait()

    steps = [(target, part) for target in range(2) for part in range(PARTS)]
    for load in loads[12:]:
        load.wait()

    def project(row, target, part):
        return dot(gated[row], cross_weight[target, row, :, part * width : (part + 1) * width])

    for target, part in steps:
        mine[target, part] = project(0, target, part)
    for copy in handed:
        copy.wait_recv()
    swap.wait_recv()
    for target, part in steps:
        send_cross[target, part] = (mine[target, part] + project(1, target, part)).astype(BF16)
        cross_copy(target, part).start()
    for part in range(2 * PARTS):
        span = slice(part * width, (part + 1) * width)
        own[:, span] = dot(gated[0], own_weight[0, :, span]) + dot(gated[1], own_weight[1, :, span])
    for part in range(PARTS):
        for source in range(2):
            span = slice(source * half + part * width, source * half + (part + 1) * width)
            cross_arrived(source, part)
            out_ref[:, span] = (own[:, span] + recv_cross[source, part].astype(F32)).astype(BF16)

    rims.wait_send()
    pl.when(core == 1)(lambda: left(send_h, 0))
    left(send_p, 1)
    left(send_y, 2)
    pltpu.make_async_copy(edge_out.at[pl.ds(0, n - 1)], edge_out.at[pl.ds(0, n - 1)], all_send.at[3]).wait()
    swap.wait_send()
    for copy in handed:
        copy.wait_send()
    for target, part in steps:
        cross_copy(target, part).wait_send()


def body(n, q_stream, k_stream, v_stream, short_taps, long_filter, skip_gain, out_weight):
    tokens, channels = long_filter.shape
    rows, features = out_weight.shape
    columns = features // lax.axis_size("chan")
    group = channels // n
    tables = transform_tables(n, tokens)
    hbm = pl.BlockSpec(memory_space=pltpu.HBM)
    operands = [
        q_stream,
        k_stream,
        v_stream,
        short_taps,
        long_filter,
        skip_gain.reshape(1, channels),
        out_weight,
        *tables,
    ]
    width = columns // 2 // PARTS
    slabs = pltpu.VMEM((n, group, tokens), BF16)
    scratch = [
        pltpu.VMEM((3, tokens, channels), BF16),
        pltpu.VMEM(short_taps.shape, F32),
        pltpu.VMEM((tokens, channels), F32),
        pltpu.VMEM((1, channels), F32),
        pltpu.VMEM((2, 2, rows, columns // 2), BF16),
        pltpu.VMEM((2, rows, columns), BF16),
        *[pltpu.VMEM(table.shape, table.dtype) for table in tables],
        pltpu.VMEM((EDGE, channels), BF16),
        pltpu.VMEM((EDGE, channels), BF16),
        pltpu.VMEM((EDGE, channels), F32),
        pltpu.VMEM((n, tokens), F32),
        pltpu.VMEM((EDGE + n, tokens), F32),
        pltpu.VMEM((3, 2 * EDGE + tokens, channels), F32),
        pltpu.VMEM((tokens, channels), F32),
        pltpu.VMEM((tokens, channels), F32),
        pltpu.VMEM((tokens, channels), F32),
        *[slabs] * 6,
        pltpu.VMEM((channels, 2 * tokens), F32),
        pltpu.VMEM((channels, tokens), F32),
        pltpu.VMEM((2, tokens, channels), BF16),
        pltpu.VMEM((2, PARTS, tokens, width), F32),
        pltpu.VMEM((tokens, columns), F32),
        pltpu.VMEM((2, PARTS, tokens, width), BF16),
        pltpu.VMEM((2, PARTS, tokens, width), BF16),
        pltpu.SemaphoreType.DMA((16,)),
        pltpu.SemaphoreType.DMA,
        pltpu.SemaphoreType.DMA,
        pltpu.SemaphoreType.DMA((4,)),
        pltpu.SemaphoreType.DMA((4,)),
        pltpu.SemaphoreType.DMA((3,)),
        pltpu.SemaphoreType.DMA((3,)),
        pltpu.SemaphoreType.DMA,
        pltpu.SemaphoreType.DMA,
        pltpu.SemaphoreType.DMA((2, PARTS)),
        pltpu.SemaphoreType.DMA((2, PARTS)),
        pltpu.SemaphoreType.REGULAR,
    ]
    return pl.pallas_call(
        functools.partial(kernel, n),
        out_shape=pltpu.VMEM((tokens, columns), BF16),
        in_specs=[hbm] * 13,
        out_specs=pl.BlockSpec(memory_space=pltpu.VMEM),
        scratch_shapes=scratch,
        compiler_params=pltpu.CompilerParams(
            collective_id=0, has_side_effects=True, vmem_limit_bytes=40 * 1024 * 1024
        ),
    )(*[pltpu.with_memory_space_constraint(jnp.asarray(each), pltpu.HBM) for each in operands])


def solution(mesh):
    in_specs = (
        P("seq", "chan"),
        P("seq", "chan"),
        P("seq", "chan"),
        P(None, None, "chan"),
        P("seq", "chan"),
        P("chan"),
        P("chan", None),
    )
    return jax.shard_map(
        functools.partial(body, mesh.shape["seq"]),
        mesh=mesh,
        in_specs=in_specs,
        out_specs=P("seq", "chan"),
        check_vma=False,
    )
```

```python
import functools
import math

import jax
import jax.numpy as jnp
import ml_dtypes
import numpy as np
from jax import lax
from jax.experimental import pallas as pl
from jax.experimental.pallas import tpu as pltpu
from jax.sharding import PartitionSpec as P

MESH = pl.DeviceIdType.MESH
F32 = jnp.float32
BF16 = jnp.bfloat16
EDGE = 8
PARTS = 2
DEPTH = 8


def transform_tables(blocks, tokens):
    length = blocks * tokens
    frequency = np.arange(blocks) + 0.25
    outer_angle = 2 * math.pi * np.outer(frequency, np.arange(blocks)) / blocks
    outer = np.concatenate([np.cos(outer_angle), np.sin(outer_angle)])
    turn = 2 * math.pi * np.outer(frequency, np.arange(tokens)) / length
    inner_angle = 2 * math.pi * np.outer(np.arange(tokens), np.arange(tokens)) / tokens
    cosine, sine = np.cos(inner_angle), np.sin(inner_angle)
    inner = np.block([[cosine, sine], [-sine, cosine]])
    back = np.block([[cosine, -sine], [sine, cosine]]) / length
    matrices = [table.astype(ml_dtypes.bfloat16) for table in (outer, outer.T.copy(), inner, back)]
    return (*matrices, np.cos(turn).astype(np.float32), np.sin(turn).astype(np.float32))


def dot(a, b):
    return jnp.dot(a, b, preferred_element_type=F32)


def kernel(
    n,
    q_hbm,
    k_hbm,
    v_hbm,
    taps_hbm,
    filter_hbm,
    skip_hbm,
    weight_hbm,
    first_hbm,
    last_hbm,
    inner_hbm,
    back_hbm,
    cos_hbm,
    sin_hbm,
    out_ref,
    streams,
    taps,
    filt,
    skip,
    cross_weight,
    own_weight,
    first,
    last,
    inner,
    back,
    cosine,
    sine,
    halo_out,
    halo_in,
    tail,
    edge_out,
    edge_in,
    padded,
    product,
    q_short,
    skipped,
    send_both,
    recv_both,
    send_y,
    recv_y,
    flat,
    gated,
    mine,
    own,
    send_cross,
    recv_cross,
    load_sem,
    halo_send,
    halo_recv,
    all_send,
    all_recv,
    weight_send,
    weight_recv,
    gated_send,
    gated_recv,
    cross_send,
    cross_recv,
):
    me, chan = lax.axis_index("seq"), lax.axis_index("chan")
    core, high = lax.rem(chan, 2), lax.div(chan, 2)
    other_core = high * 2 + 1 - core
    across = ((1 - high) * 2 + 1, (1 - high) * 2)
    tokens, channels = filt.shape
    group = channels // n
    columns = own_weight.shape[2]

    half = columns // 2

    def weight_part(feature_block, start, width):
        return weight_hbm.at[:, pl.ds(pl.multiple_of(feature_block * columns + start, half), width)]

    def parts_for(which):
        return [
            weight_part((1 - high) * 2 + 1, which * half, half),
            weight_part((1 - high) * 2, which * half, half),
            weight_part(high * 2 + which, 0, columns),
        ]

    def weight_slots(row):
        return [cross_weight.at[0, row], cross_weight.at[1, row], own_weight.at[row]]

    pairs = [
        (k_hbm, streams.at[1]),
        (v_hbm, streams.at[2]),
        (taps_hbm, taps),
        (filter_hbm, filt),
        (q_hbm, streams.at[0]),
        (skip_hbm, skip),
        (first_hbm, first),
        (cos_hbm, cosine),
        (sin_hbm, sine),
        (inner_hbm, inner),
        (back_hbm, back),
        (last_hbm, last),
        *zip(parts_for(core), weight_slots(0)),
    ]
    loads = [pltpu.make_async_copy(src, dst, load_sem.at[i]) for i, (src, dst) in enumerate(pairs)]
    for load in loads[:6]:
        load.start()

    def rounds(send):
        place, depth = lax.div(me, DEPTH), lax.rem(me, DEPTH)
        row, pair = lax.div(place, 2), lax.rem(place, 2)
        for step_row, step_pair in ((2, 1), (2, 0), (1, 1), (3, 1), (1, 0), (3, 0), (0, 1), (0, 0)):
            line = (lax.rem(row + step_row, n // DEPTH // 2) * 2 + lax.rem(pair + step_pair, 2)) * DEPTH

            @pl.loop(0, DEPTH if step_row + step_pair else DEPTH - 1)
            def _(i):
                far = DEPTH // 2 - lax.div(i + 1, 2)
                step = jnp.where(lax.rem(i, 2) == 1, far, DEPTH - far)
                send(line + lax.rem(depth + step, DEPTH))

    barrier = pltpu.get_barrier_semaphore()

    def greet(peer):
        pl.semaphore_signal(barrier, inc=1, device_id=(peer, chan), device_id_type=MESH)

    rounds(greet)
    for neighbour in (other_core, *across):
        pl.semaphore_signal(barrier, inc=1, device_id=(me, neighbour), device_id_type=MESH)
    for load in loads[6:12]:
        load.start()

    def exchange(*routes):
        def send(peer):
            for source, target, index in routes:
                pltpu.make_async_remote_copy(
                    src_ref=source(peer),
                    dst_ref=target(me),
                    send_sem=all_send.at[index],
                    recv_sem=all_recv.at[index],
                    device_id=(peer, chan),
                    device_id_type=MESH,
                ).start()

        rounds(send)

    def slabs(source, target, index):
        return (lambda peer: source.at[peer], lambda own_place: target.at[own_place], index)

    edges = (
        lambda peer: edge_out.at[pl.ds(peer, 1)],
        lambda own_place: edge_in.at[pl.ds(edge + own_place, 1)],
        1,
    )

    def arrived(buffer, index):
        part = buffer.at[pl.ds(0, n - 1)]
        pltpu.make_async_copy(part, part, all_recv.at[index]).wait()

    def left(buffer, index):
        part = buffer.at[pl.ds(0, n - 1)]
        pltpu.make_async_copy(part, part, all_send.at[index]).wait()

    edge = EDGE

    def short(i, first_row, rows):
        start = edge + first_row
        total = taps[i, 0:1] * padded[i, start : start + rows]
        for lag in range(1, taps.shape[1]):
            total += taps[i, lag : lag + 1] * padded[i, start - lag : start - lag + rows]
        return total

    def fill(i):
        padded[i, 0:edge] = jnp.zeros((edge, channels), F32)
        padded[i, edge : edge + tokens] = streams[i].astype(F32)
        padded[i, edge + tokens :] = jnp.zeros((edge, channels), F32)

    for load in loads[0:3]:
        load.wait()
    fill(1)
    fill(2)
    k_short, v_short = short(1, 0, tokens), short(2, 0, tokens)
    product[...] = k_short * v_short
    rim = taps.shape[1] - 1
    for i, value in enumerate((k_short, v_short, short(1, tokens, edge), short(2, tokens, edge))):
        tail[i * rim : (i + 1) * rim] = value[:rim]
    for i in range(channels // tokens):
        flat[0, i * tokens : (i + 1) * tokens, 0:edge] = tail[:, i * tokens : (i + 1) * tokens].T
    pieces = [flat[0, pl.ds(c, n, stride=group)][:, 0:edge] for c in range(group)]
    edge_out[:, 0 : group * edge] = jnp.concatenate(pieces, axis=1)
    edge_out[:, group * edge :] = jnp.zeros((n, tokens - group * edge), F32)
    edge_in[0:edge] = jnp.zeros((edge, tokens), F32)
    loads[3].wait()
    per = tokens // group
    for i in range(channels // tokens):
        both = [value[:, i * tokens : (i + 1) * tokens].T.reshape(per, group, tokens) for value in (filt, product)]
        send_both[i * per : (i + 1) * per] = jnp.concatenate(both, axis=1).astype(BF16)
    loads[4].wait()
    fill(0)

    tail[...] = jnp.zeros(tail.shape, F32)
    for i in range(3):
        tail[i * rim : (i + 1) * rim] = padded[i, edge + tokens - rim : edge + tokens]
    halo_out[...] = tail[...].astype(BF16)

    pl.semaphore_wait(barrier, n + 2)
    rims = pltpu.make_async_remote_copy(
        src_ref=halo_out,
        dst_ref=halo_in,
        send_sem=halo_send,
        recv_sem=halo_recv,
        device_id=(lax.rem(me + 1, n), chan),
        device_id_type=MESH,
    )
    exchange(slabs(send_both, recv_both, 0), edges)
    rims.start()
    recv_both[me] = send_both[me]
    edge_in[pl.ds(edge + me, 1)] = edge_out[pl.ds(me, 1)]
    for load in loads[12:]:
        load.start()
    handed = []
    for i, (src, dst) in enumerate(zip(parts_for(1 - core), weight_slots(1))):
        handed.append(
            pltpu.make_async_remote_copy(
                src_ref=src,
                dst_ref=dst,
                send_sem=weight_send.at[i],
                recv_sem=weight_recv.at[i],
                device_id=(me, other_core),
                device_id_type=MESH,
            )
        )
        handed[-1].start()
    for load in loads[6:12]:
        load.wait()

    def forward(which, heads=None):
        slab = recv_both[...].astype(F32)[:, which * group : (which + 1) * group]
        flat[which] = slab.reshape(channels, tokens)
        signal = [flat[which, pl.ds(c, n, stride=group)] for c in range(group)]
        if heads is not None:
            first_lanes = lax.broadcasted_iota(jnp.int32, (n, tokens), 1) < rim
            moved = [pltpu.roll(heads, (tokens - c * edge) % tokens, axis=1) for c in range(group)]
            signal = [jnp.where(first_lanes, new, old) for new, old in zip(moved, signal)]
        signal = [value.astype(BF16) for value in signal]
        stage = dot(first[...], jnp.concatenate(signal, axis=1))
        turned = []
        for c in range(group):
            real, imag = stage[:n, c * tokens : (c + 1) * tokens], stage[n:, c * tokens : (c + 1) * tokens]
            pair = [real * cosine[...] - imag * sine[...], real * sine[...] + imag * cosine[...]]
            turned.append(jnp.concatenate(pair, axis=1).astype(BF16))
        return dot(jnp.concatenate(turned, axis=0), inner[...])

    arrived(recv_both, 0)
    pltpu.make_async_copy(edge_in.at[pl.ds(0, n - 1)], edge_in.at[pl.ds(0, n - 1)], all_recv.at[1]).wait()
    before = pltpu.roll(edge_in[edge - 1 : edge - 1 + n], tokens - 2 * rim, axis=1)
    completed = edge_in[edge : edge + n] + before
    heads = completed * pltpu.roll(completed, tokens - rim, axis=1)
    response = forward(0)
    spectrum = forward(1, heads)
    p_real, p_imag = spectrum[:, :tokens], spectrum[:, tokens:]
    h_real, h_imag = response[:, :tokens], response[:, tokens:]
    filtered = [p_real * h_real - p_imag * h_imag, p_real * h_imag + p_imag * h_real]
    mixed = dot(jnp.concatenate(filtered, axis=1).astype(BF16), back[...])
    turned = []
    for c in range(group):
        real, imag = mixed[c * n : (c + 1) * n, :tokens], mixed[c * n : (c + 1) * n, tokens:]
        pair = [real * cosine[...] + imag * sine[...], imag * cosine[...] - real * sine[...]]
        turned.append(jnp.concatenate(pair, axis=0).astype(BF16))
    convolved = dot(last[...], jnp.concatenate(turned, axis=1))
    for c in range(group):
        flat[0, pl.ds(c, n, stride=group)] = convolved[:, c * tokens : (c + 1) * tokens]
    send_y[...] = flat[0].reshape(n, group, tokens).astype(BF16)
    exchange(slabs(send_y, recv_y, 2))
    recv_y[me] = send_y[me]
    loads[5].wait()
    rims.wait_recv()
    inside = jnp.where(me > 0, 1.0, 0.0).astype(F32)
    tail[...] = halo_in[...].astype(F32) * inside
    for i in range(3):
        padded[i, edge - rim : edge] = tail[i * rim : (i + 1) * rim]
    product[0:edge] = short(1, 0, edge) * short(2, 0, edge)
    skipped[...] = skip[...] * product[...]
    q_short[...] = short(0, 0, tokens)
    arrived(recv_y, 2)

    long_part = recv_y[...].astype(F32).reshape(channels, tokens)
    long_part = jnp.concatenate([long_part[i * tokens : (i + 1) * tokens].T for i in range(channels // tokens)], axis=1)
    gated[0] = (q_short[...] * (long_part + skipped[...])).astype(BF16)
    swap = pltpu.make_async_remote_copy(
        src_ref=gated.at[0],
        dst_ref=gated.at[1],
        send_sem=gated_send,
        recv_sem=gated_recv,
        device_id=(me, other_core),
        device_id_type=MESH,
    )
    swap.start()

    width = half // PARTS

    def cross_copy(target, part):
        return pltpu.make_async_remote_copy(
            src_ref=send_cross.at[target, part],
            dst_ref=recv_cross.at[core, part],
            send_sem=cross_send.at[target, part],
            recv_sem=cross_recv.at[core, part],
            device_id=(me, across[target]),
            device_id_type=MESH,
        )

    def cross_arrived(source, part):
        pltpu.make_async_copy(recv_cross.at[source, part], recv_cross.at[source, part], cross_recv.at[source, part]).wait()

    steps = [(target, part) for target in range(2) for part in range(PARTS)]
    for load in loads[12:]:
        load.wait()

    def project(row, target, part):
        return dot(gated[row], cross_weight[target, row, :, part * width : (part + 1) * width])

    lead = steps[0]
    mine[lead] = project(0, *lead)
    for copy in handed:
        copy.wait_recv()
    swap.wait_recv()
    for target, part in steps:
        early = mine[lead] if (target, part) == lead else project(0, target, part)
        send_cross[target, part] = (early + project(1, target, part)).astype(BF16)
        cross_copy(target, part).start()
    for part in range(2 * PARTS):
        span = slice(part * width, (part + 1) * width)
        own[:, span] = dot(gated[0], own_weight[0, :, span]) + dot(gated[1], own_weight[1, :, span])
    for part in range(PARTS):
        for source in range(2):
            span = slice(source * half + part * width, source * half + (part + 1) * width)
            cross_arrived(source, part)
            out_ref[:, span] = (own[:, span] + recv_cross[source, part].astype(F32)).astype(BF16)

    rims.wait_send()
    left(send_both, 0)
    left(send_y, 2)
    pltpu.make_async_copy(edge_out.at[pl.ds(0, n - 1)], edge_out.at[pl.ds(0, n - 1)], all_send.at[1]).wait()
    swap.wait_send()
    for copy in handed:
        copy.wait_send()
    for target, part in steps:
        cross_copy(target, part).wait_send()


def body(n, q_stream, k_stream, v_stream, short_taps, long_filter, skip_gain, out_weight):
    tokens, channels = long_filter.shape
    rows, features = out_weight.shape
    columns = features // lax.axis_size("chan")
    group = channels // n
    tables = transform_tables(n, tokens)
    hbm = pl.BlockSpec(memory_space=pltpu.HBM)
    operands = [
        q_stream,
        k_stream,
        v_stream,
        short_taps,
        long_filter,
        skip_gain.reshape(1, channels),
        out_weight,
        *tables,
    ]
    width = columns // 2 // PARTS
    slabs = pltpu.VMEM((n, group, tokens), BF16)
    scratch = [
        pltpu.VMEM((3, tokens, channels), BF16),
        pltpu.VMEM(short_taps.shape, F32),
        pltpu.VMEM((tokens, channels), F32),
        pltpu.VMEM((1, channels), F32),
        pltpu.VMEM((2, 2, rows, columns // 2), BF16),
        pltpu.VMEM((2, rows, columns), BF16),
        *[pltpu.VMEM(table.shape, table.dtype) for table in tables],
        pltpu.VMEM((EDGE, channels), BF16),
        pltpu.VMEM((EDGE, channels), BF16),
        pltpu.VMEM((EDGE, channels), F32),
        pltpu.VMEM((n, tokens), F32),
        pltpu.VMEM((EDGE + n, tokens), F32),
        pltpu.VMEM((3, 2 * EDGE + tokens, channels), F32),
        pltpu.VMEM((tokens, channels), F32),
        pltpu.VMEM((tokens, channels), F32),
        pltpu.VMEM((tokens, channels), F32),
        *[pltpu.VMEM((n, 2 * group, tokens), BF16)] * 2,
        *[slabs] * 2,
        pltpu.VMEM((2, channels, tokens), F32),
        pltpu.VMEM((2, tokens, channels), BF16),
        pltpu.VMEM((2, PARTS, tokens, width), F32),
        pltpu.VMEM((tokens, columns), F32),
        pltpu.VMEM((2, PARTS, tokens, width), BF16),
        pltpu.VMEM((2, PARTS, tokens, width), BF16),
        pltpu.SemaphoreType.DMA((16,)),
        pltpu.SemaphoreType.DMA,
        pltpu.SemaphoreType.DMA,
        pltpu.SemaphoreType.DMA((3,)),
        pltpu.SemaphoreType.DMA((3,)),
        pltpu.SemaphoreType.DMA((3,)),
        pltpu.SemaphoreType.DMA((3,)),
        pltpu.SemaphoreType.DMA,
        pltpu.SemaphoreType.DMA,
        pltpu.SemaphoreType.DMA((2, PARTS)),
        pltpu.SemaphoreType.DMA((2, PARTS)),
    ]
    return pl.pallas_call(
        functools.partial(kernel, n),
        out_shape=pltpu.VMEM((tokens, columns), BF16),
        in_specs=[hbm] * 13,
        out_specs=pl.BlockSpec(memory_space=pltpu.VMEM),
        scratch_shapes=scratch,
        compiler_params=pltpu.CompilerParams(
            collective_id=0, has_side_effects=True, vmem_limit_bytes=40 * 1024 * 1024
        ),
    )(*[pltpu.with_memory_space_constraint(jnp.asarray(each), pltpu.HBM) for each in operands])


def solution(mesh):
    in_specs = (
        P("seq", "chan"),
        P("seq", "chan"),
        P("seq", "chan"),
        P(None, None, "chan"),
        P("seq", "chan"),
        P("chan"),
        P("chan", None),
    )
    return jax.shard_map(
        functools.partial(body, mesh.shape["seq"]),
        mesh=mesh,
        in_specs=in_specs,
        out_specs=P("seq", "chan"),
        check_vma=False,
    )
```

```python
import functools
import math

import jax
import jax.numpy as jnp
import ml_dtypes
import numpy as np
from jax import lax
from jax.experimental import pallas as pl
from jax.experimental.pallas import tpu as pltpu
from jax.sharding import PartitionSpec as P

MESH = pl.DeviceIdType.MESH
F32 = jnp.float32
BF16 = jnp.bfloat16
EDGE = 8
PARTS = 2
DEPTH = 8
SPLIT = 2


def narrow(table):
    return table.astype(ml_dtypes.bfloat16)


def in_two(table, axis):
    high = narrow(table)
    return np.concatenate([high, narrow(table - high.astype(np.float64))], axis=axis)


def twice(value, axis):
    return jnp.concatenate([value, value], axis=axis)


def transform_tables(blocks, tokens):
    length = blocks * tokens
    frequency = np.arange(blocks) + 0.25
    outer_angle = 2 * math.pi * np.outer(frequency, np.arange(blocks)) / blocks
    outer = np.concatenate([np.cos(outer_angle), np.sin(outer_angle)])
    turn = 2 * math.pi * np.outer(frequency, np.arange(tokens)) / length
    inner_angle = 2 * math.pi * np.outer(np.arange(tokens), np.arange(tokens)) / tokens
    cosine, sine = np.cos(inner_angle), np.sin(inner_angle)
    inner = np.block([[cosine, sine], [-sine, cosine]])
    back = np.block([[cosine, -sine], [sine, cosine]]) / length
    matrices = [in_two(outer, 1), in_two(outer.T, 1), narrow(inner), narrow(back)]
    return (*matrices, np.cos(turn).astype(np.float32), np.sin(turn).astype(np.float32))


def dot(a, b):
    return jnp.dot(a, b, preferred_element_type=F32)


def kernel(
    n,
    q_hbm,
    k_hbm,
    v_hbm,
    taps_hbm,
    filter_hbm,
    skip_hbm,
    weight_hbm,
    first_hbm,
    last_hbm,
    inner_hbm,
    back_hbm,
    cos_hbm,
    sin_hbm,
    out_ref,
    streams,
    taps,
    filt,
    skip,
    cross_weight,
    own_weight,
    first,
    last,
    inner,
    back,
    cosine,
    sine,
    halo_out,
    halo_in,
    tail,
    edge_out,
    edge_in,
    padded,
    product,
    q_short,
    skipped,
    send_both,
    recv_both,
    send_y,
    recv_y,
    flat,
    gated,
    mine,
    own,
    send_cross,
    recv_cross,
    load_sem,
    halo_send,
    halo_recv,
    all_send,
    all_recv,
    weight_send,
    weight_recv,
    gated_send,
    gated_recv,
    cross_send,
    cross_recv,
    turn_sem,
):
    me, chan = lax.axis_index("seq"), lax.axis_index("chan")
    core, high = lax.rem(chan, 2), lax.div(chan, 2)
    other_core = high * 2 + 1 - core
    across = ((1 - high) * 2 + 1, (1 - high) * 2)
    tokens, channels = filt.shape
    group = channels // n
    columns = own_weight.shape[2]

    half = columns // 2

    def weight_part(feature_block, start, width):
        return weight_hbm.at[:, pl.ds(pl.multiple_of(feature_block * columns + start, half), width)]

    def parts_for(which):
        return [
            weight_part((1 - high) * 2 + 1, which * half, half),
            weight_part((1 - high) * 2, which * half, half),
            weight_part(high * 2 + which, 0, columns),
        ]

    def weight_slots(row):
        return [cross_weight.at[0, row], cross_weight.at[1, row], own_weight.at[row]]

    pairs = [
        (k_hbm, streams.at[1]),
        (v_hbm, streams.at[2]),
        (taps_hbm, taps),
        (filter_hbm, filt),
        (q_hbm, streams.at[0]),
        (skip_hbm, skip),
        (first_hbm, first),
        (cos_hbm, cosine),
        (sin_hbm, sine),
        (inner_hbm, inner),
        (back_hbm, back),
        (last_hbm, last),
        *zip(parts_for(core), weight_slots(0)),
    ]
    loads = [pltpu.make_async_copy(src, dst, load_sem.at[i]) for i, (src, dst) in enumerate(pairs)]
    for load in loads[:6]:
        load.start()

    lines = ((2, 1), (2, 0), (1, 1), (3, 1), (1, 0), (3, 0), (0, 1), (0, 0))

    def rounds(send, chosen=lines):
        place, depth = lax.div(me, DEPTH), lax.rem(me, DEPTH)
        row, pair = lax.div(place, 2), lax.rem(place, 2)
        for step_row, step_pair in chosen:
            line = (lax.rem(row + step_row, n // DEPTH // 2) * 2 + lax.rem(pair + step_pair, 2)) * DEPTH

            @pl.loop(0, DEPTH if step_row + step_pair else DEPTH - 1)
            def _(i):
                far = DEPTH // 2 - lax.div(i + 1, 2)
                step = jnp.where(lax.rem(i, 2) == 1, far, DEPTH - far)
                send(line + lax.rem(depth + step, DEPTH))

    barrier = pltpu.get_barrier_semaphore()

    def greet(peer):
        pl.semaphore_signal(barrier, inc=1, device_id=(peer, chan), device_id_type=MESH)

    rounds(greet)
    for neighbour in (other_core, *across):
        pl.semaphore_signal(barrier, inc=1, device_id=(me, neighbour), device_id_type=MESH)
    for load in loads[6:12]:
        load.start()

    def exchange(*routes, chosen=lines):
        def send(peer):
            for source, target, index, leaves in routes:
                pltpu.make_async_remote_copy(
                    src_ref=source(peer),
                    dst_ref=target(me),
                    send_sem=all_send.at[leaves],
                    recv_sem=all_recv.at[index],
                    device_id=(peer, chan),
                    device_id_type=MESH,
                ).start()

        rounds(send, chosen)

    def slabs(source, target, index, leaves):
        return (lambda peer: source.at[peer], lambda own_place: target.at[own_place], index, leaves)

    edges = (
        lambda peer: edge_out.at[pl.ds(peer, 1)],
        lambda own_place: edge_in.at[pl.ds(edge + own_place, 1)],
        1,
        1,
    )

    def arrived(buffer, index):
        part = buffer.at[pl.ds(0, n - 1)]
        pltpu.make_async_copy(part, part, all_recv.at[index]).wait()

    def left(buffer, index, count):
        part = buffer.at[pl.ds(0, count)]
        pltpu.make_async_copy(part, part, all_send.at[index]).wait()

    edge = EDGE

    def short(i, first_row, rows):
        start = edge + first_row
        total = taps[i, 0:1] * padded[i, start : start + rows]
        for lag in range(1, taps.shape[1]):
            total += taps[i, lag : lag + 1] * padded[i, start - lag : start - lag + rows]
        return total

    def fill(i):
        padded[i, 0:edge] = jnp.zeros((edge, channels), F32)
        padded[i, edge : edge + tokens] = streams[i].astype(F32)
        padded[i, edge + tokens :] = jnp.zeros((edge, channels), F32)

    for load in loads[0:3]:
        load.wait()
    fill(1)
    fill(2)
    k_short, v_short = short(1, 0, tokens), short(2, 0, tokens)
    product[...] = k_short * v_short
    rim = taps.shape[1] - 1
    for i, value in enumerate((k_short, v_short, short(1, tokens, edge), short(2, tokens, edge))):
        tail[i * rim : (i + 1) * rim] = value[:rim]
    for i in range(channels // tokens):
        flat[0, i * tokens : (i + 1) * tokens, 0:edge] = tail[:, i * tokens : (i + 1) * tokens].T
    pieces = [flat[0, pl.ds(c, n, stride=group)][:, 0:edge] for c in range(group)]
    edge_out[:, 0 : group * edge] = jnp.concatenate(pieces, axis=1)
    edge_out[:, group * edge :] = jnp.zeros((n, tokens - group * edge), F32)
    edge_in[0:edge] = jnp.zeros((edge, tokens), F32)
    loads[3].wait()
    per = tokens // group
    for i in range(channels // tokens):
        both = [value[:, i * tokens : (i + 1) * tokens].T.reshape(per, group, tokens) for value in (filt, product)]
        send_both[i * per : (i + 1) * per] = jnp.concatenate(both, axis=1).astype(BF16)
    loads[4].wait()
    fill(0)

    tail[...] = jnp.zeros(tail.shape, F32)
    for i in range(3):
        tail[i * rim : (i + 1) * rim] = padded[i, edge + tokens - rim : edge + tokens]
    halo_out[...] = tail[...].astype(BF16)

    pl.semaphore_wait(barrier, n + 2)
    rims = pltpu.make_async_remote_copy(
        src_ref=halo_out,
        dst_ref=halo_in,
        send_sem=halo_send,
        recv_sem=halo_recv,
        device_id=(lax.rem(me + 1, n), chan),
        device_id_type=MESH,
    )
    exchange(slabs(send_both, recv_both, 0, 0), edges, chosen=lines[:SPLIT])

    @pl.when(core == 1)
    def _():
        pl.semaphore_wait(turn_sem, 1)

    exchange(slabs(send_both, recv_both, 0, 3), edges, chosen=lines[SPLIT:])

    @pl.when(core == 0)
    def _():
        left(send_both, 0, SPLIT * DEPTH)
        pl.semaphore_signal(turn_sem, inc=1, device_id=(me, other_core), device_id_type=MESH)

    rims.start()
    recv_both[me] = send_both[me]
    edge_in[pl.ds(edge + me, 1)] = edge_out[pl.ds(me, 1)]
    for load in loads[12:]:
        load.start()
    handed = []
    for i, (src, dst) in enumerate(zip(parts_for(1 - core), weight_slots(1))):
        handed.append(
            pltpu.make_async_remote_copy(
                src_ref=src,
                dst_ref=dst,
                send_sem=weight_send.at[i],
                recv_sem=weight_recv.at[i],
                device_id=(me, other_core),
                device_id_type=MESH,
            )
        )
        handed[-1].start()
    for load in loads[6:12]:
        load.wait()

    def forward(which, heads=None):
        slab = recv_both[...].astype(F32)[:, which * group : (which + 1) * group]
        flat[which] = slab.reshape(channels, tokens)
        signal = [flat[which, pl.ds(c, n, stride=group)] for c in range(group)]
        if heads is not None:
            first_lanes = lax.broadcasted_iota(jnp.int32, (n, tokens), 1) < rim
            moved = [pltpu.roll(heads, (tokens - c * edge) % tokens, axis=1) for c in range(group)]
            signal = [jnp.where(first_lanes, new, old) for new, old in zip(moved, signal)]
        signal = [value.astype(BF16) for value in signal]
        stage = dot(first[...], twice(jnp.concatenate(signal, axis=1), 0))
        turned = []
        for c in range(group):
            real, imag = stage[:n, c * tokens : (c + 1) * tokens], stage[n:, c * tokens : (c + 1) * tokens]
            pair = [real * cosine[...] - imag * sine[...], real * sine[...] + imag * cosine[...]]
            turned.append(jnp.concatenate(pair, axis=1).astype(BF16))
        return dot(jnp.concatenate(turned, axis=0), inner[...])

    arrived(recv_both, 0)
    pltpu.make_async_copy(edge_in.at[pl.ds(0, n - 1)], edge_in.at[pl.ds(0, n - 1)], all_recv.at[1]).wait()
    before = pltpu.roll(edge_in[edge - 1 : edge - 1 + n], tokens - 2 * rim, axis=1)
    completed = edge_in[edge : edge + n] + before
    heads = completed * pltpu.roll(completed, tokens - rim, axis=1)
    response = forward(0)
    spectrum = forward(1, heads)
    p_real, p_imag = spectrum[:, :tokens], spectrum[:, tokens:]
    h_real, h_imag = response[:, :tokens], response[:, tokens:]
    filtered = [p_real * h_real - p_imag * h_imag, p_real * h_imag + p_imag * h_real]
    mixed = dot(jnp.concatenate(filtered, axis=1).astype(BF16), back[...])
    turned = []
    for c in range(group):
        real, imag = mixed[c * n : (c + 1) * n, :tokens], mixed[c * n : (c + 1) * n, tokens:]
        pair = [real * cosine[...] + imag * sine[...], imag * cosine[...] - real * sine[...]]
        turned.append(jnp.concatenate(pair, axis=0).astype(BF16))
    convolved = dot(last[...], twice(jnp.concatenate(turned, axis=1), 0))
    for c in range(group):
        flat[0, pl.ds(c, n, stride=group)] = convolved[:, c * tokens : (c + 1) * tokens]
    send_y[...] = flat[0].reshape(n, group, tokens).astype(BF16)
    exchange(slabs(send_y, recv_y, 2, 2))
    recv_y[me] = send_y[me]
    loads[5].wait()
    rims.wait_recv()
    inside = jnp.where(me > 0, 1.0, 0.0).astype(F32)
    tail[...] = halo_in[...].astype(F32) * inside
    for i in range(3):
        padded[i, edge - rim : edge] = tail[i * rim : (i + 1) * rim]
    product[0:edge] = short(1, 0, edge) * short(2, 0, edge)
    skipped[...] = skip[...] * product[...]
    q_short[...] = short(0, 0, tokens)
    arrived(recv_y, 2)

    long_part = recv_y[...].astype(F32).reshape(channels, tokens)
    long_part = jnp.concatenate([long_part[i * tokens : (i + 1) * tokens].T for i in range(channels // tokens)], axis=1)
    gated[0] = (q_short[...] * (long_part + skipped[...])).astype(BF16)
    swap = pltpu.make_async_remote_copy(
        src_ref=gated.at[0],
        dst_ref=gated.at[1],
        send_sem=gated_send,
        recv_sem=gated_recv,
        device_id=(me, other_core),
        device_id_type=MESH,
    )
    swap.start()

    width = half // PARTS

    def cross_copy(target, part):
        return pltpu.make_async_remote_copy(
            src_ref=send_cross.at[target, part],
            dst_ref=recv_cross.at[core, part],
            send_sem=cross_send.at[target, part],
            recv_sem=cross_recv.at[core, part],
            device_id=(me, across[target]),
            device_id_type=MESH,
        )

    def cross_arrived(source, part):
        pltpu.make_async_copy(recv_cross.at[source, part], recv_cross.at[source, part], cross_recv.at[source, part]).wait()

    steps = [(target, part) for target in range(2) for part in range(PARTS)]
    for load in loads[12:]:
        load.wait()

    def project(row, target, part):
        return dot(gated[row], cross_weight[target, row, :, part * width : (part + 1) * width])

    lead = steps[0]
    mine[lead] = project(0, *lead)
    for copy in handed:
        copy.wait_recv()
    swap.wait_recv()
    for target, part in steps:
        early = mine[lead] if (target, part) == lead else project(0, target, part)
        send_cross[target, part] = (early + project(1, target, part)).astype(BF16)
        cross_copy(target, part).start()
    for part in range(2 * PARTS):
        span = slice(part * width, (part + 1) * width)
        own[:, span] = dot(gated[0], own_weight[0, :, span]) + dot(gated[1], own_weight[1, :, span])
    for part in range(PARTS):
        for source in range(2):
            span = slice(source * half + part * width, source * half + (part + 1) * width)
            cross_arrived(source, part)
            out_ref[:, span] = (own[:, span] + recv_cross[source, part].astype(F32)).astype(BF16)

    rims.wait_send()
    pl.when(core == 1)(lambda: left(send_both, 0, SPLIT * DEPTH))
    left(send_both, 3, n - 1 - SPLIT * DEPTH)
    left(send_y, 2, n - 1)
    pltpu.make_async_copy(edge_out.at[pl.ds(0, n - 1)], edge_out.at[pl.ds(0, n - 1)], all_send.at[1]).wait()
    swap.wait_send()
    for copy in handed:
        copy.wait_send()
    for target, part in steps:
        cross_copy(target, part).wait_send()


def body(n, q_stream, k_stream, v_stream, short_taps, long_filter, skip_gain, out_weight):
    tokens, channels = long_filter.shape
    rows, features = out_weight.shape
    columns = features // lax.axis_size("chan")
    group = channels // n
    tables = transform_tables(n, tokens)
    hbm = pl.BlockSpec(memory_space=pltpu.HBM)
    operands = [
        q_stream,
        k_stream,
        v_stream,
        short_taps,
        long_filter,
        skip_gain.reshape(1, channels),
        out_weight,
        *tables,
    ]
    width = columns // 2 // PARTS
    slabs = pltpu.VMEM((n, group, tokens), BF16)
    scratch = [
        pltpu.VMEM((3, tokens, channels), BF16),
        pltpu.VMEM(short_taps.shape, F32),
        pltpu.VMEM((tokens, channels), F32),
        pltpu.VMEM((1, channels), F32),
        pltpu.VMEM((2, 2, rows, columns // 2), BF16),
        pltpu.VMEM((2, rows, columns), BF16),
        *[pltpu.VMEM(table.shape, table.dtype) for table in tables],
        pltpu.VMEM((EDGE, channels), BF16),
        pltpu.VMEM((EDGE, channels), BF16),
        pltpu.VMEM((EDGE, channels), F32),
        pltpu.VMEM((n, tokens), F32),
        pltpu.VMEM((EDGE + n, tokens), F32),
        pltpu.VMEM((3, 2 * EDGE + tokens, channels), F32),
        pltpu.VMEM((tokens, channels), F32),
        pltpu.VMEM((tokens, channels), F32),
        pltpu.VMEM((tokens, channels), F32),
        *[pltpu.VMEM((n, 2 * group, tokens), BF16)] * 2,
        *[slabs] * 2,
        pltpu.VMEM((2, channels, tokens), F32),
        pltpu.VMEM((2, tokens, channels), BF16),
        pltpu.VMEM((2, PARTS, tokens, width), F32),
        pltpu.VMEM((tokens, columns), F32),
        pltpu.VMEM((2, PARTS, tokens, width), BF16),
        pltpu.VMEM((2, PARTS, tokens, width), BF16),
        pltpu.SemaphoreType.DMA((16,)),
        pltpu.SemaphoreType.DMA,
        pltpu.SemaphoreType.DMA,
        pltpu.SemaphoreType.DMA((4,)),
        pltpu.SemaphoreType.DMA((3,)),
        pltpu.SemaphoreType.DMA((3,)),
        pltpu.SemaphoreType.DMA((3,)),
        pltpu.SemaphoreType.DMA,
        pltpu.SemaphoreType.DMA,
        pltpu.SemaphoreType.DMA((2, PARTS)),
        pltpu.SemaphoreType.DMA((2, PARTS)),
        pltpu.SemaphoreType.REGULAR,
    ]
    return pl.pallas_call(
        functools.partial(kernel, n),
        out_shape=pltpu.VMEM((tokens, columns), BF16),
        in_specs=[hbm] * 13,
        out_specs=pl.BlockSpec(memory_space=pltpu.VMEM),
        scratch_shapes=scratch,
        compiler_params=pltpu.CompilerParams(
            collective_id=0, has_side_effects=True, vmem_limit_bytes=40 * 1024 * 1024
        ),
    )(*[pltpu.with_memory_space_constraint(jnp.asarray(each), pltpu.HBM) for each in operands])


def solution(mesh):
    in_specs = (
        P("seq", "chan"),
        P("seq", "chan"),
        P("seq", "chan"),
        P(None, None, "chan"),
        P("seq", "chan"),
        P("chan"),
        P("chan", None),
    )
    return jax.shard_map(
        functools.partial(body, mesh.shape["seq"]),
        mesh=mesh,
        in_specs=in_specs,
        out_specs=P("seq", "chan"),
        check_vma=False,
    )
```

```python
import functools
import math

import jax
import jax.numpy as jnp
import ml_dtypes
import numpy as np
from jax import lax
from jax.experimental import pallas as pl
from jax.experimental.pallas import tpu as pltpu
from jax.sharding import PartitionSpec as P

MESH = pl.DeviceIdType.MESH
F32 = jnp.float32
BF16 = jnp.bfloat16
EDGE = 8
PARTS = 2
DEPTH = 8
SPLIT = 2


def narrow(table):
    return table.astype(ml_dtypes.bfloat16)


def in_two(table, axis):
    high = narrow(table)
    return np.concatenate([high, narrow(table - high.astype(np.float64))], axis=axis)


def twice(value, axis):
    return jnp.concatenate([value, value], axis=axis)


def transform_tables(blocks, tokens):
    length = blocks * tokens
    frequency = np.arange(blocks) + 0.25
    outer_angle = 2 * math.pi * np.outer(frequency, np.arange(blocks)) / blocks
    outer = np.concatenate([np.cos(outer_angle), np.sin(outer_angle)])
    turn = 2 * math.pi * np.outer(frequency, np.arange(tokens)) / length
    inner_angle = 2 * math.pi * np.outer(np.arange(tokens), np.arange(tokens)) / tokens
    cosine, sine = np.cos(inner_angle), np.sin(inner_angle)
    inner = np.block([[cosine, sine], [-sine, cosine]])
    back = np.block([[cosine, -sine], [sine, cosine]]) / length
    matrices = [in_two(outer, 1), in_two(outer.T, 1), narrow(inner), narrow(back)]
    return (*matrices, np.cos(turn).astype(np.float32), np.sin(turn).astype(np.float32))


def dot(a, b):
    return jnp.dot(a, b, preferred_element_type=F32)


def kernel(
    n,
    q_hbm,
    k_hbm,
    v_hbm,
    taps_hbm,
    filter_hbm,
    skip_hbm,
    weight_hbm,
    first_hbm,
    last_hbm,
    inner_hbm,
    back_hbm,
    cos_hbm,
    sin_hbm,
    out_ref,
    streams,
    taps,
    filt,
    skip,
    cross_weight,
    own_weight,
    first,
    last,
    inner,
    back,
    cosine,
    sine,
    halo_out,
    halo_in,
    tail,
    edge_out,
    edge_in,
    padded,
    product,
    q_short,
    skipped,
    send_both,
    recv_both,
    send_y,
    recv_y,
    flat,
    gated,
    mine,
    own,
    send_cross,
    recv_cross,
    load_sem,
    halo_send,
    halo_recv,
    all_send,
    all_recv,
    weight_send,
    weight_recv,
    gated_send,
    gated_recv,
    cross_send,
    cross_recv,
    turn_sem,
):
    me, chan = lax.axis_index("seq"), lax.axis_index("chan")
    core, high = lax.rem(chan, 2), lax.div(chan, 2)
    other_core = high * 2 + 1 - core
    across = ((1 - high) * 2 + 1, (1 - high) * 2)
    tokens, channels = filt.shape
    group = channels // n
    columns = own_weight.shape[2]

    half = columns // 2

    def weight_part(feature_block, start, width):
        return weight_hbm.at[:, pl.ds(pl.multiple_of(feature_block * columns + start, half), width)]

    def parts_for(which):
        return [
            weight_part((1 - high) * 2 + 1, which * half, half),
            weight_part((1 - high) * 2, which * half, half),
            weight_part(high * 2 + which, 0, columns),
        ]

    def weight_slots(row):
        return [cross_weight.at[0, row], cross_weight.at[1, row], own_weight.at[row]]

    pairs = [
        (k_hbm, streams.at[1]),
        (v_hbm, streams.at[2]),
        (taps_hbm, taps),
        (filter_hbm, filt),
        (q_hbm, streams.at[0]),
        (skip_hbm, skip),
        (first_hbm, first),
        (cos_hbm, cosine),
        (sin_hbm, sine),
        (inner_hbm, inner),
        (back_hbm, back),
        (last_hbm, last),
        *zip(parts_for(core), weight_slots(0)),
    ]
    loads = [pltpu.make_async_copy(src, dst, load_sem.at[i]) for i, (src, dst) in enumerate(pairs)]
    for load in loads[:6]:
        load.start()

    lines = ((2, 1), (2, 0), (1, 1), (3, 1), (1, 0), (3, 0), (0, 1), (0, 0))

    def rounds(send, chosen=lines):
        place, depth = lax.div(me, DEPTH), lax.rem(me, DEPTH)
        row, pair = lax.div(place, 2), lax.rem(place, 2)
        for step_row, step_pair in chosen:
            line = (lax.rem(row + step_row, n // DEPTH // 2) * 2 + lax.rem(pair + step_pair, 2)) * DEPTH

            @pl.loop(0, DEPTH if step_row + step_pair else DEPTH - 1)
            def _(i):
                far = DEPTH // 2 - lax.div(i + 1, 2)
                step = jnp.where(lax.rem(i, 2) == 1, far, DEPTH - far)
                send(line + lax.rem(depth + step, DEPTH))

    barrier = pltpu.get_barrier_semaphore()

    def greet(peer):
        pl.semaphore_signal(barrier, inc=1, device_id=(peer, chan), device_id_type=MESH)

    rounds(greet)
    for neighbour in (other_core, *across):
        pl.semaphore_signal(barrier, inc=1, device_id=(me, neighbour), device_id_type=MESH)
    for load in loads[6:12]:
        load.start()

    def exchange(*routes, chosen=lines):
        def send(peer):
            for source, target, index, leaves in routes:
                pltpu.make_async_remote_copy(
                    src_ref=source(peer),
                    dst_ref=target(me),
                    send_sem=all_send.at[leaves],
                    recv_sem=all_recv.at[index],
                    device_id=(peer, chan),
                    device_id_type=MESH,
                ).start()

        rounds(send, chosen)

    def slabs(source, target, index, leaves):
        return (lambda peer: source.at[peer], lambda own_place: target.at[own_place], index, leaves)

    edges = (
        lambda peer: edge_out.at[pl.ds(peer, 1)],
        lambda own_place: edge_in.at[pl.ds(edge + own_place, 1)],
        1,
        1,
    )

    def arrived(buffer, index):
        part = buffer.at[pl.ds(0, n - 1)]
        pltpu.make_async_copy(part, part, all_recv.at[index]).wait()

    def left(buffer, index, count):
        part = buffer.at[pl.ds(0, count)]
        pltpu.make_async_copy(part, part, all_send.at[index]).wait()

    edge = EDGE

    def short(i, first_row, rows):
        start = edge + first_row
        total = taps[i, 0:1] * padded[i, start : start + rows]
        for lag in range(1, taps.shape[1]):
            total += taps[i, lag : lag + 1] * padded[i, start - lag : start - lag + rows]
        return total

    def fill(i):
        padded[i, 0:edge] = jnp.zeros((edge, channels), F32)
        padded[i, edge : edge + tokens] = streams[i].astype(F32)
        padded[i, edge + tokens :] = jnp.zeros((edge, channels), F32)

    for load in loads[0:3]:
        load.wait()
    fill(1)
    fill(2)
    k_short, v_short = short(1, 0, tokens), short(2, 0, tokens)
    product[...] = k_short * v_short
    rim = taps.shape[1] - 1
    for i, value in enumerate((k_short, v_short, short(1, tokens, edge), short(2, tokens, edge))):
        tail[i * rim : (i + 1) * rim] = value[:rim]
    for i in range(channels // tokens):
        flat[0, i * tokens : (i + 1) * tokens, 0:edge] = tail[:, i * tokens : (i + 1) * tokens].T
    pieces = [flat[0, pl.ds(c, n, stride=group)][:, 0:edge] for c in range(group)]
    edge_out[:, 0 : group * edge] = jnp.concatenate(pieces, axis=1)
    edge_out[:, group * edge :] = jnp.zeros((n, tokens - group * edge), F32)
    edge_in[0:edge] = jnp.zeros((edge, tokens), F32)
    loads[3].wait()
    per = tokens // group
    for i in range(channels // tokens):
        both = [value[:, i * tokens : (i + 1) * tokens].T.reshape(per, group, tokens) for value in (filt, product)]
        send_both[i * per : (i + 1) * per] = jnp.concatenate(both, axis=1).astype(BF16)
    loads[4].wait()
    fill(0)

    tail[...] = jnp.zeros(tail.shape, F32)
    for i in range(3):
        tail[i * rim : (i + 1) * rim] = padded[i, edge + tokens - rim : edge + tokens]
    halo_out[...] = tail[...].astype(BF16)

    pl.semaphore_wait(barrier, n + 2)
    rims = pltpu.make_async_remote_copy(
        src_ref=halo_out,
        dst_ref=halo_in,
        send_sem=halo_send,
        recv_sem=halo_recv,
        device_id=(lax.rem(me + 1, n), chan),
        device_id_type=MESH,
    )
    exchange(slabs(send_both, recv_both, 0, 0), edges, chosen=lines[:SPLIT])

    @pl.when(core == 1)
    def _():
        pl.semaphore_wait(turn_sem, 1)

    exchange(slabs(send_both, recv_both, 0, 3), edges, chosen=lines[SPLIT:])

    @pl.when(core == 0)
    def _():
        left(send_both, 0, SPLIT * DEPTH)
        pl.semaphore_signal(turn_sem, inc=1, device_id=(me, other_core), device_id_type=MESH)

    rims.start()
    recv_both[me] = send_both[me]
    edge_in[pl.ds(edge + me, 1)] = edge_out[pl.ds(me, 1)]
    for load in loads[12:]:
        load.start()
    handed = []
    for i, (src, dst) in enumerate(zip(parts_for(1 - core), weight_slots(1))):
        handed.append(
            pltpu.make_async_remote_copy(
                src_ref=src,
                dst_ref=dst,
                send_sem=weight_send.at[i],
                recv_sem=weight_recv.at[i],
                device_id=(me, other_core),
                device_id_type=MESH,
            )
        )
        handed[-1].start()
    for load in loads[6:12]:
        load.wait()

    def forward(which, heads=None):
        slab = recv_both[...].astype(F32)[:, which * group : (which + 1) * group]
        flat[which] = slab.reshape(channels, tokens)
        signal = [flat[which, pl.ds(c, n, stride=group)] for c in range(group)]
        if heads is not None:
            first_lanes = lax.broadcasted_iota(jnp.int32, (n, tokens), 1) < rim
            moved = [pltpu.roll(heads, (tokens - c * edge) % tokens, axis=1) for c in range(group)]
            signal = [jnp.where(first_lanes, new, old) for new, old in zip(moved, signal)]
        signal = [value.astype(BF16) for value in signal]
        stage = dot(first[...], twice(jnp.concatenate(signal, axis=1), 0))
        turned = []
        for c in range(group):
            real, imag = stage[:n, c * tokens : (c + 1) * tokens], stage[n:, c * tokens : (c + 1) * tokens]
            pair = [real * cosine[...] - imag * sine[...], real * sine[...] + imag * cosine[...]]
            turned.append(jnp.concatenate(pair, axis=1).astype(BF16))
        return dot(jnp.concatenate(turned, axis=0), inner[...])

    arrived(recv_both, 0)
    pltpu.make_async_copy(edge_in.at[pl.ds(0, n - 1)], edge_in.at[pl.ds(0, n - 1)], all_recv.at[1]).wait()
    before = pltpu.roll(edge_in[edge - 1 : edge - 1 + n], tokens - 2 * rim, axis=1)
    completed = edge_in[edge : edge + n] + before
    heads = completed * pltpu.roll(completed, tokens - rim, axis=1)
    response = forward(0)
    spectrum = forward(1, heads)
    p_real, p_imag = spectrum[:, :tokens], spectrum[:, tokens:]
    h_real, h_imag = response[:, :tokens], response[:, tokens:]
    filtered = [p_real * h_real - p_imag * h_imag, p_real * h_imag + p_imag * h_real]
    mixed = dot(jnp.concatenate(filtered, axis=1).astype(BF16), back[...])
    turned = []
    for c in range(group):
        real, imag = mixed[c * n : (c + 1) * n, :tokens], mixed[c * n : (c + 1) * n, tokens:]
        pair = [real * cosine[...] + imag * sine[...], imag * cosine[...] - real * sine[...]]
        turned.append(jnp.concatenate(pair, axis=0).astype(BF16))
    convolved = dot(last[...], twice(jnp.concatenate(turned, axis=1), 0))
    for c in range(group):
        flat[0, pl.ds(c, n, stride=group)] = convolved[:, c * tokens : (c + 1) * tokens]
    send_y[...] = flat[0].reshape(n, group, tokens).astype(BF16)
    exchange(slabs(send_y, recv_y, 2, 2))
    recv_y[me] = send_y[me]
    loads[5].wait()
    rims.wait_recv()
    inside = jnp.where(me > 0, 1.0, 0.0).astype(F32)
    tail[...] = halo_in[...].astype(F32) * inside
    for i in range(3):
        padded[i, edge - rim : edge] = tail[i * rim : (i + 1) * rim]
    product[0:edge] = short(1, 0, edge) * short(2, 0, edge)
    skipped[...] = skip[...] * product[...]
    q_short[...] = short(0, 0, tokens)
    arrived(recv_y, 2)

    long_part = recv_y[...].astype(F32).reshape(channels, tokens)
    swaps = []
    for i in range(channels // tokens):
        span = slice(i * tokens, (i + 1) * tokens)
        gated[0, :, span] = (q_short[:, span] * (long_part[span].T + skipped[:, span])).astype(BF16)
        swaps.append(
            pltpu.make_async_remote_copy(
                src_ref=gated.at[0, :, pl.ds(i * tokens, tokens)],
                dst_ref=gated.at[1, :, pl.ds(i * tokens, tokens)],
                send_sem=gated_send.at[i],
                recv_sem=gated_recv.at[i],
                device_id=(me, other_core),
                device_id_type=MESH,
            )
        )
        swaps[-1].start()

    width = half // PARTS

    def cross_copy(target, part):
        return pltpu.make_async_remote_copy(
            src_ref=send_cross.at[target, part],
            dst_ref=recv_cross.at[core, part],
            send_sem=cross_send.at[target, part],
            recv_sem=cross_recv.at[core, part],
            device_id=(me, across[target]),
            device_id_type=MESH,
        )

    def cross_arrived(source, part):
        pltpu.make_async_copy(recv_cross.at[source, part], recv_cross.at[source, part], cross_recv.at[source, part]).wait()

    steps = [(target, part) for target in range(2) for part in range(PARTS)]
    for load in loads[12:]:
        load.wait()

    def project(row, target, part):
        return dot(gated[row], cross_weight[target, row, :, part * width : (part + 1) * width])

    lead = steps[0]
    mine[lead] = project(0, *lead)
    for copy in handed:
        copy.wait_recv()
    for swap in swaps:
        swap.wait_recv()
    for target, part in steps:
        early = mine[lead] if (target, part) == lead else project(0, target, part)
        send_cross[target, part] = (early + project(1, target, part)).astype(BF16)
        cross_copy(target, part).start()
    for part in range(2 * PARTS):
        span = slice(part * width, (part + 1) * width)
        own[:, span] = dot(gated[0], own_weight[0, :, span]) + dot(gated[1], own_weight[1, :, span])
    for part in range(PARTS):
        for source in range(2):
            span = slice(source * half + part * width, source * half + (part + 1) * width)
            cross_arrived(source, part)
            out_ref[:, span] = (own[:, span] + recv_cross[source, part].astype(F32)).astype(BF16)

    rims.wait_send()
    pl.when(core == 1)(lambda: left(send_both, 0, SPLIT * DEPTH))
    left(send_both, 3, n - 1 - SPLIT * DEPTH)
    left(send_y, 2, n - 1)
    pltpu.make_async_copy(edge_out.at[pl.ds(0, n - 1)], edge_out.at[pl.ds(0, n - 1)], all_send.at[1]).wait()
    for swap in swaps:
        swap.wait_send()
    for copy in handed:
        copy.wait_send()
    for target, part in steps:
        cross_copy(target, part).wait_send()


def body(n, q_stream, k_stream, v_stream, short_taps, long_filter, skip_gain, out_weight):
    tokens, channels = long_filter.shape
    rows, features = out_weight.shape
    columns = features // lax.axis_size("chan")
    group = channels // n
    tables = transform_tables(n, tokens)
    hbm = pl.BlockSpec(memory_space=pltpu.HBM)
    operands = [
        q_stream,
        k_stream,
        v_stream,
        short_taps,
        long_filter,
        skip_gain.reshape(1, channels),
        out_weight,
        *tables,
    ]
    width = columns // 2 // PARTS
    slabs = pltpu.VMEM((n, group, tokens), BF16)
    scratch = [
        pltpu.VMEM((3, tokens, channels), BF16),
        pltpu.VMEM(short_taps.shape, F32),
        pltpu.VMEM((tokens, channels), F32),
        pltpu.VMEM((1, channels), F32),
        pltpu.VMEM((2, 2, rows, columns // 2), BF16),
        pltpu.VMEM((2, rows, columns), BF16),
        *[pltpu.VMEM(table.shape, table.dtype) for table in tables],
        pltpu.VMEM((EDGE, channels), BF16),
        pltpu.VMEM((EDGE, channels), BF16),
        pltpu.VMEM((EDGE, channels), F32),
        pltpu.VMEM((n, tokens), F32),
        pltpu.VMEM((EDGE + n, tokens), F32),
        pltpu.VMEM((3, 2 * EDGE + tokens, channels), F32),
        pltpu.VMEM((tokens, channels), F32),
        pltpu.VMEM((tokens, channels), F32),
        pltpu.VMEM((tokens, channels), F32),
        *[pltpu.VMEM((n, 2 * group, tokens), BF16)] * 2,
        *[slabs] * 2,
        pltpu.VMEM((2, channels, tokens), F32),
        pltpu.VMEM((2, tokens, channels), BF16),
        pltpu.VMEM((2, PARTS, tokens, width), F32),
        pltpu.VMEM((tokens, columns), F32),
        pltpu.VMEM((2, PARTS, tokens, width), BF16),
        pltpu.VMEM((2, PARTS, tokens, width), BF16),
        pltpu.SemaphoreType.DMA((16,)),
        pltpu.SemaphoreType.DMA,
        pltpu.SemaphoreType.DMA,
        pltpu.SemaphoreType.DMA((4,)),
        pltpu.SemaphoreType.DMA((3,)),
        pltpu.SemaphoreType.DMA((3,)),
        pltpu.SemaphoreType.DMA((3,)),
        pltpu.SemaphoreType.DMA((channels // tokens,)),
        pltpu.SemaphoreType.DMA((channels // tokens,)),
        pltpu.SemaphoreType.DMA((2, PARTS)),
        pltpu.SemaphoreType.DMA((2, PARTS)),
        pltpu.SemaphoreType.REGULAR,
    ]
    return pl.pallas_call(
        functools.partial(kernel, n),
        out_shape=pltpu.VMEM((tokens, columns), BF16),
        in_specs=[hbm] * 13,
        out_specs=pl.BlockSpec(memory_space=pltpu.VMEM),
        scratch_shapes=scratch,
        compiler_params=pltpu.CompilerParams(
            collective_id=0, has_side_effects=True, vmem_limit_bytes=40 * 1024 * 1024
        ),
    )(*[pltpu.with_memory_space_constraint(jnp.asarray(each), pltpu.HBM) for each in operands])


def solution(mesh):
    in_specs = (
        P("seq", "chan"),
        P("seq", "chan"),
        P("seq", "chan"),
        P(None, None, "chan"),
        P("seq", "chan"),
        P("chan"),
        P("chan", None),
    )
    return jax.shard_map(
        functools.partial(body, mesh.shape["seq"]),
        mesh=mesh,
        in_specs=in_specs,
        out_specs=P("seq", "chan"),
        check_vma=False,
    )
```

```python
import functools
import math

import jax
import jax.numpy as jnp
import ml_dtypes
import numpy as np
from jax import lax
from jax.experimental import pallas as pl
from jax.experimental.pallas import tpu as pltpu
from jax.sharding import PartitionSpec as P

MESH = pl.DeviceIdType.MESH
F32 = jnp.float32
BF16 = jnp.bfloat16
EDGE = 8
PARTS = 2
DEPTH = 8
SPLIT = 2


def narrow(table):
    return table.astype(ml_dtypes.bfloat16)


def in_two(table, axis):
    high = narrow(table)
    return np.concatenate([high, narrow(table - high.astype(np.float64))], axis=axis)


def twice(value, axis):
    return jnp.concatenate([value, value], axis=axis)


def transform_tables(blocks, tokens):
    length = blocks * tokens
    frequency = np.arange(blocks) + 0.25
    outer_angle = 2 * math.pi * np.outer(frequency, np.arange(blocks)) / blocks
    outer = np.concatenate([np.cos(outer_angle), np.sin(outer_angle)])
    turn = 2 * math.pi * np.outer(frequency, np.arange(tokens)) / length
    inner_angle = 2 * math.pi * np.outer(np.arange(tokens), np.arange(tokens)) / tokens
    cosine, sine = np.cos(inner_angle), np.sin(inner_angle)
    inner = np.block([[cosine, sine], [-sine, cosine]])
    back = np.block([[cosine, -sine], [sine, cosine]]) / length
    matrices = [in_two(outer, 1), in_two(outer.T, 1), narrow(inner), narrow(back)]
    return (*matrices, np.cos(turn).astype(np.float32), np.sin(turn).astype(np.float32))


def dot(a, b):
    return jnp.dot(a, b, preferred_element_type=F32)


def kernel(
    n,
    q_hbm,
    k_hbm,
    v_hbm,
    taps_hbm,
    filter_hbm,
    skip_hbm,
    weight_hbm,
    first_hbm,
    last_hbm,
    inner_hbm,
    back_hbm,
    cos_hbm,
    sin_hbm,
    out_ref,
    streams,
    taps,
    filt,
    skip,
    cross_weight,
    own_weight,
    first,
    last,
    inner,
    back,
    cosine,
    sine,
    halo_out,
    halo_in,
    tail,
    edge_out,
    edge_in,
    padded,
    product,
    q_short,
    skipped,
    send_both,
    recv_both,
    send_y,
    recv_y,
    flat,
    gated,
    mine,
    own,
    send_cross,
    recv_cross,
    load_sem,
    halo_send,
    halo_recv,
    all_send,
    all_recv,
    weight_send,
    weight_recv,
    gated_send,
    gated_recv,
    cross_send,
    cross_recv,
    turn_sem,
):
    me, chan = lax.axis_index("seq"), lax.axis_index("chan")
    core, high = lax.rem(chan, 2), lax.div(chan, 2)
    other_core = high * 2 + 1 - core
    across = ((1 - high) * 2 + 1, (1 - high) * 2)
    tokens, channels = filt.shape
    group = channels // n
    columns = own_weight.shape[2]

    half = columns // 2

    def weight_part(feature_block, start, width):
        return weight_hbm.at[:, pl.ds(pl.multiple_of(feature_block * columns + start, half), width)]

    def parts_for(which):
        return [
            weight_part((1 - high) * 2 + 1, which * half, half),
            weight_part((1 - high) * 2, which * half, half),
            weight_part(high * 2 + which, 0, columns),
        ]

    def weight_slots(row):
        return [cross_weight.at[0, row], cross_weight.at[1, row], own_weight.at[row]]

    pairs = [
        (k_hbm, streams.at[1]),
        (v_hbm, streams.at[2]),
        (taps_hbm, taps),
        (filter_hbm, filt),
        (q_hbm, streams.at[0]),
        (skip_hbm, skip),
        (first_hbm, first),
        (cos_hbm, cosine),
        (sin_hbm, sine),
        (inner_hbm, inner),
        (back_hbm, back),
        (last_hbm, last),
        *zip(parts_for(core), weight_slots(0)),
    ]
    loads = [pltpu.make_async_copy(src, dst, load_sem.at[i]) for i, (src, dst) in enumerate(pairs)]

    lines = ((2, 1), (2, 0), (1, 1), (3, 1), (1, 0), (3, 0), (0, 1), (0, 0))

    def rounds(send, chosen=lines):
        place, depth = lax.div(me, DEPTH), lax.rem(me, DEPTH)
        row, pair = lax.div(place, 2), lax.rem(place, 2)
        for step_row, step_pair in chosen:
            line = (lax.rem(row + step_row, n // DEPTH // 2) * 2 + lax.rem(pair + step_pair, 2)) * DEPTH

            @pl.loop(0, DEPTH if step_row + step_pair else DEPTH - 1)
            def _(i):
                far = DEPTH // 2 - lax.div(i + 1, 2)
                step = jnp.where(lax.rem(i, 2) == 1, far, DEPTH - far)
                send(line + lax.rem(depth + step, DEPTH))

    barrier = pltpu.get_barrier_semaphore()

    def greet(peer):
        pl.semaphore_signal(barrier, inc=1, device_id=(peer, chan), device_id_type=MESH)

    rounds(greet)
    for load in loads[:6]:
        load.start()
    for neighbour in (other_core, *across):
        pl.semaphore_signal(barrier, inc=1, device_id=(me, neighbour), device_id_type=MESH)
    for load in loads[6:12]:
        load.start()

    def exchange(*routes, chosen=lines):
        def send(peer):
            for source, target, index, leaves in routes:
                pltpu.make_async_remote_copy(
                    src_ref=source(peer),
                    dst_ref=target(me),
                    send_sem=all_send.at[leaves],
                    recv_sem=all_recv.at[index],
                    device_id=(peer, chan),
                    device_id_type=MESH,
                ).start()

        rounds(send, chosen)

    def slabs(source, target, index, leaves):
        return (lambda peer: source.at[peer], lambda own_place: target.at[own_place], index, leaves)

    edges = (
        lambda peer: edge_out.at[pl.ds(peer, 1)],
        lambda own_place: edge_in.at[pl.ds(edge + own_place, 1)],
        1,
        1,
    )

    def arrived(buffer, index):
        part = buffer.at[pl.ds(0, n - 1)]
        pltpu.make_async_copy(part, part, all_recv.at[index]).wait()

    def left(buffer, index, count):
        part = buffer.at[pl.ds(0, count)]
        pltpu.make_async_copy(part, part, all_send.at[index]).wait()

    edge = EDGE

    def short(i, first_row, rows):
        start = edge + first_row
        total = taps[i, 0:1] * padded[i, start : start + rows]
        for lag in range(1, taps.shape[1]):
            total += taps[i, lag : lag + 1] * padded[i, start - lag : start - lag + rows]
        return total

    def fill(i):
        padded[i, 0:edge] = jnp.zeros((edge, channels), F32)
        padded[i, edge : edge + tokens] = streams[i].astype(F32)
        padded[i, edge + tokens :] = jnp.zeros((edge, channels), F32)

    for load in loads[0:3]:
        load.wait()
    fill(1)
    fill(2)
    k_short, v_short = short(1, 0, tokens), short(2, 0, tokens)
    product[...] = k_short * v_short
    rim = taps.shape[1] - 1
    for i, value in enumerate((k_short, v_short, short(1, tokens, edge), short(2, tokens, edge))):
        tail[i * rim : (i + 1) * rim] = value[:rim]
    for i in range(channels // tokens):
        flat[0, i * tokens : (i + 1) * tokens, 0:edge] = tail[:, i * tokens : (i + 1) * tokens].T
    pieces = [flat[0, pl.ds(c, n, stride=group)][:, 0:edge] for c in range(group)]
    edge_out[:, 0 : group * edge] = jnp.concatenate(pieces, axis=1)
    edge_out[:, group * edge :] = jnp.zeros((n, tokens - group * edge), F32)
    edge_in[0:edge] = jnp.zeros((edge, tokens), F32)
    loads[3].wait()
    per = tokens // group
    for i in range(channels // tokens):
        both = [value[:, i * tokens : (i + 1) * tokens].T.reshape(per, group, tokens) for value in (filt, product)]
        send_both[i * per : (i + 1) * per] = jnp.concatenate(both, axis=1).astype(BF16)
    loads[4].wait()
    fill(0)

    tail[...] = jnp.zeros(tail.shape, F32)
    for i in range(3):
        tail[i * rim : (i + 1) * rim] = padded[i, edge + tokens - rim : edge + tokens]
    halo_out[...] = tail[...].astype(BF16)

    pl.semaphore_wait(barrier, n + 2)
    rims = pltpu.make_async_remote_copy(
        src_ref=halo_out,
        dst_ref=halo_in,
        send_sem=halo_send,
        recv_sem=halo_recv,
        device_id=(lax.rem(me + 1, n), chan),
        device_id_type=MESH,
    )
    exchange(slabs(send_both, recv_both, 0, 0), edges, chosen=lines[:SPLIT])

    @pl.when(core == 1)
    def _():
        pl.semaphore_wait(turn_sem, 1)

    exchange(slabs(send_both, recv_both, 0, 3), edges, chosen=lines[SPLIT:])

    @pl.when(core == 0)
    def _():
        left(send_both, 0, SPLIT * DEPTH)
        pl.semaphore_signal(turn_sem, inc=1, device_id=(me, other_core), device_id_type=MESH)

    rims.start()
    recv_both[me] = send_both[me]
    edge_in[pl.ds(edge + me, 1)] = edge_out[pl.ds(me, 1)]
    for load in loads[12:]:
        load.start()
    handed = []
    for i, (src, dst) in enumerate(zip(parts_for(1 - core), weight_slots(1))):
        handed.append(
            pltpu.make_async_remote_copy(
                src_ref=src,
                dst_ref=dst,
                send_sem=weight_send.at[i],
                recv_sem=weight_recv.at[i],
                device_id=(me, other_core),
                device_id_type=MESH,
            )
        )
        handed[-1].start()
    for load in loads[6:12]:
        load.wait()

    def forward(which, heads=None):
        slab = recv_both[...].astype(F32)[:, which * group : (which + 1) * group]
        flat[which] = slab.reshape(channels, tokens)
        signal = [flat[which, pl.ds(c, n, stride=group)] for c in range(group)]
        if heads is not None:
            first_lanes = lax.broadcasted_iota(jnp.int32, (n, tokens), 1) < rim
            moved = [pltpu.roll(heads, (tokens - c * edge) % tokens, axis=1) for c in range(group)]
            signal = [jnp.where(first_lanes, new, old) for new, old in zip(moved, signal)]
        signal = [value.astype(BF16) for value in signal]
        stage = dot(first[...], twice(jnp.concatenate(signal, axis=1), 0))
        turned = []
        for c in range(group):
            real, imag = stage[:n, c * tokens : (c + 1) * tokens], stage[n:, c * tokens : (c + 1) * tokens]
            pair = [real * cosine[...] - imag * sine[...], real * sine[...] + imag * cosine[...]]
            turned.append(jnp.concatenate(pair, axis=1).astype(BF16))
        return dot(jnp.concatenate(turned, axis=0), inner[...])

    arrived(recv_both, 0)
    pltpu.make_async_copy(edge_in.at[pl.ds(0, n - 1)], edge_in.at[pl.ds(0, n - 1)], all_recv.at[1]).wait()
    before = pltpu.roll(edge_in[edge - 1 : edge - 1 + n], tokens - 2 * rim, axis=1)
    completed = edge_in[edge : edge + n] + before
    heads = completed * pltpu.roll(completed, tokens - rim, axis=1)
    response = forward(0)
    spectrum = forward(1, heads)
    p_real, p_imag = spectrum[:, :tokens], spectrum[:, tokens:]
    h_real, h_imag = response[:, :tokens], response[:, tokens:]
    filtered = [p_real * h_real - p_imag * h_imag, p_real * h_imag + p_imag * h_real]
    mixed = dot(jnp.concatenate(filtered, axis=1).astype(BF16), back[...])
    turned = []
    for c in range(group):
        real, imag = mixed[c * n : (c + 1) * n, :tokens], mixed[c * n : (c + 1) * n, tokens:]
        pair = [real * cosine[...] + imag * sine[...], imag * cosine[...] - real * sine[...]]
        turned.append(jnp.concatenate(pair, axis=0).astype(BF16))
    convolved = dot(last[...], twice(jnp.concatenate(turned, axis=1), 0))
    for c in range(group):
        flat[0, pl.ds(c, n, stride=group)] = convolved[:, c * tokens : (c + 1) * tokens]
    send_y[...] = flat[0].reshape(n, group, tokens).astype(BF16)
    exchange(slabs(send_y, recv_y, 2, 2))
    recv_y[me] = send_y[me]
    loads[5].wait()
    rims.wait_recv()
    inside = jnp.where(me > 0, 1.0, 0.0).astype(F32)
    tail[...] = halo_in[...].astype(F32) * inside
    for i in range(3):
        padded[i, edge - rim : edge] = tail[i * rim : (i + 1) * rim]
    product[0:edge] = short(1, 0, edge) * short(2, 0, edge)
    skipped[...] = skip[...] * product[...]
    q_short[...] = short(0, 0, tokens)
    arrived(recv_y, 2)

    long_part = recv_y[...].astype(F32).reshape(channels, tokens)
    swaps = []
    for i in range(channels // tokens):
        span = slice(i * tokens, (i + 1) * tokens)
        gated[0, :, span] = (q_short[:, span] * (long_part[span].T + skipped[:, span])).astype(BF16)
        swaps.append(
            pltpu.make_async_remote_copy(
                src_ref=gated.at[0, :, pl.ds(i * tokens, tokens)],
                dst_ref=gated.at[1, :, pl.ds(i * tokens, tokens)],
                send_sem=gated_send.at[i],
                recv_sem=gated_recv.at[i],
                device_id=(me, other_core),
                device_id_type=MESH,
            )
        )
        swaps[-1].start()

    width = half // PARTS

    def cross_copy(target, part):
        return pltpu.make_async_remote_copy(
            src_ref=send_cross.at[target, part],
            dst_ref=recv_cross.at[core, part],
            send_sem=cross_send.at[target, part],
            recv_sem=cross_recv.at[core, part],
            device_id=(me, across[target]),
            device_id_type=MESH,
        )

    def cross_arrived(source, part):
        pltpu.make_async_copy(recv_cross.at[source, part], recv_cross.at[source, part], cross_recv.at[source, part]).wait()

    steps = [(target, part) for target in range(2) for part in range(PARTS)]
    for load in loads[12:]:
        load.wait()

    def project(row, target, part):
        return dot(gated[row], cross_weight[target, row, :, part * width : (part + 1) * width])

    lead = steps[0]
    mine[lead] = project(0, *lead)
    for copy in handed:
        copy.wait_recv()
    for swap in swaps:
        swap.wait_recv()
    for target, part in steps:
        early = mine[lead] if (target, part) == lead else project(0, target, part)
        send_cross[target, part] = (early + project(1, target, part)).astype(BF16)
        cross_copy(target, part).start()
    for part in range(2 * PARTS):
        span = slice(part * width, (part + 1) * width)
        own[:, span] = dot(gated[0], own_weight[0, :, span]) + dot(gated[1], own_weight[1, :, span])
    for part in range(PARTS):
        for source in range(2):
            span = slice(source * half + part * width, source * half + (part + 1) * width)
            cross_arrived(source, part)
            out_ref[:, span] = (own[:, span] + recv_cross[source, part].astype(F32)).astype(BF16)

    rims.wait_send()
    pl.when(core == 1)(lambda: left(send_both, 0, SPLIT * DEPTH))
    left(send_both, 3, n - 1 - SPLIT * DEPTH)
    left(send_y, 2, n - 1)
    pltpu.make_async_copy(edge_out.at[pl.ds(0, n - 1)], edge_out.at[pl.ds(0, n - 1)], all_send.at[1]).wait()
    for swap in swaps:
        swap.wait_send()
    for copy in handed:
        copy.wait_send()
    for target, part in steps:
        cross_copy(target, part).wait_send()


def body(n, q_stream, k_stream, v_stream, short_taps, long_filter, skip_gain, out_weight):
    tokens, channels = long_filter.shape
    rows, features = out_weight.shape
    columns = features // lax.axis_size("chan")
    group = channels // n
    tables = transform_tables(n, tokens)
    hbm = pl.BlockSpec(memory_space=pltpu.HBM)
    operands = [
        q_stream,
        k_stream,
        v_stream,
        short_taps,
        long_filter,
        skip_gain.reshape(1, channels),
        out_weight,
        *tables,
    ]
    width = columns // 2 // PARTS
    slabs = pltpu.VMEM((n, group, tokens), BF16)
    scratch = [
        pltpu.VMEM((3, tokens, channels), BF16),
        pltpu.VMEM(short_taps.shape, F32),
        pltpu.VMEM((tokens, channels), F32),
        pltpu.VMEM((1, channels), F32),
        pltpu.VMEM((2, 2, rows, columns // 2), BF16),
        pltpu.VMEM((2, rows, columns), BF16),
        *[pltpu.VMEM(table.shape, table.dtype) for table in tables],
        pltpu.VMEM((EDGE, channels), BF16),
        pltpu.VMEM((EDGE, channels), BF16),
        pltpu.VMEM((EDGE, channels), F32),
        pltpu.VMEM((n, tokens), F32),
        pltpu.VMEM((EDGE + n, tokens), F32),
        pltpu.VMEM((3, 2 * EDGE + tokens, channels), F32),
        pltpu.VMEM((tokens, channels), F32),
        pltpu.VMEM((tokens, channels), F32),
        pltpu.VMEM((tokens, channels), F32),
        *[pltpu.VMEM((n, 2 * group, tokens), BF16)] * 2,
        *[slabs] * 2,
        pltpu.VMEM((2, channels, tokens), F32),
        pltpu.VMEM((2, tokens, channels), BF16),
        pltpu.VMEM((2, PARTS, tokens, width), F32),
        pltpu.VMEM((tokens, columns), F32),
        pltpu.VMEM((2, PARTS, tokens, width), BF16),
        pltpu.VMEM((2, PARTS, tokens, width), BF16),
        pltpu.SemaphoreType.DMA((16,)),
        pltpu.SemaphoreType.DMA,
        pltpu.SemaphoreType.DMA,
        pltpu.SemaphoreType.DMA((4,)),
        pltpu.SemaphoreType.DMA((3,)),
        pltpu.SemaphoreType.DMA((3,)),
        pltpu.SemaphoreType.DMA((3,)),
        pltpu.SemaphoreType.DMA((channels // tokens,)),
        pltpu.SemaphoreType.DMA((channels // tokens,)),
        pltpu.SemaphoreType.DMA((2, PARTS)),
        pltpu.SemaphoreType.DMA((2, PARTS)),
        pltpu.SemaphoreType.REGULAR,
    ]
    return pl.pallas_call(
        functools.partial(kernel, n),
        out_shape=pltpu.VMEM((tokens, columns), BF16),
        in_specs=[hbm] * 13,
        out_specs=pl.BlockSpec(memory_space=pltpu.VMEM),
        scratch_shapes=scratch,
        compiler_params=pltpu.CompilerParams(
            collective_id=0, has_side_effects=True, vmem_limit_bytes=40 * 1024 * 1024
        ),
    )(*[pltpu.with_memory_space_constraint(jnp.asarray(each), pltpu.HBM) for each in operands])


def solution(mesh):
    in_specs = (
        P("seq", "chan"),
        P("seq", "chan"),
        P("seq", "chan"),
        P(None, None, "chan"),
        P("seq", "chan"),
        P("chan"),
        P("chan", None),
    )
    return jax.shard_map(
        functools.partial(body, mesh.shape["seq"]),
        mesh=mesh,
        in_specs=in_specs,
        out_specs=P("seq", "chan"),
        check_vma=False,
    )
```
